512 devices in a mesh: row: 2 (over y_hi), grp: 4 (over x), sec: 64 (over z, y_lo, core).
Axes of the slice: x: 4, y: 4 (y_hi: 2, y_lo: 2; y = y_hi * 2 + y_lo), z: 16, core: 2. Of those that a mesh axis runs over, the one named last changes fastest.
Arguments:
- state: float32 [2, 5, 1024, 8192], P('row', None, 'grp', 'sec'), may hold values from -6 to 6
- damping: float32 [2, 1024, 8192], P('row', 'grp', 'sec'), may hold values from 0.1 to 1
- jac_axial: float32 [2, 5, 5], P('row'), may hold values from -2.5 to 2.5
- jac_angular: float32 [2, 5, 5], P('row'), may hold values from -2.5 to 2.5
- section_shift: int32 [3], replicated, may hold values from 0 to 63, as said below
- donor_offset: int32 [8192], replicated, may hold values from 0 to 3
- match_weight: float32 [4, 8192], replicated, may hold values from 0.1 to 1
Outputs:
- advanced: float32 [2, 5, 1024, 8192], P('row', None, 'grp', 'sec')
The draws below stay inside these ranges and needn't reach their ends.
Inputs may be any that keep to these rules, and one draw needn't show every extreme that they name: `section_shift`: whole-sector rotation of the rotor against the stator at each section; one section shifts by 32 sectors and another by 64 - 1.
All inputs are finite; a program needn't handle non-finite values.
Results may differ from the reference program's by a relative error of at most 0.00002.
Values sent between devices are 32-bit elements; how exact they have to be, the bound alone decides.
No kernel may reach another device: no remote copies, remote signals or barrier semaphores. Data moves between devices by JAX's collectives and lax.ppermute only.
A program may use at most 64 MiB of HBM per device.

```python
import math
import jax
import jax.numpy as jnp
from jax import lax

CT = 128
FIELDS = 5
DONORS = 4
OFFSETS = 4
NQ = 1024
NT = 8192
N_SEC = 64


def draw_section_shift(key, part):
    key = jax.random.fold_in(key, 7)
    key_values, key_first, key_second = jax.random.split(key, 3)
    values = jax.random.randint(key_values, (3,), 0, N_SEC).astype(jnp.int32)
    first_slot = jax.random.randint(key_first, (), 0, 3).astype(jnp.int32)
    second_slot = ((first_slot + 1 + jax.random.randint(key_second, (), 0, 2)) % 3).astype(jnp.int32)
    slots = jnp.arange(3, dtype=jnp.int32)
    values = jnp.where(slots == first_slot, jnp.int32(N_SEC // 2), values)
    values = jnp.where(slots == second_slot, jnp.int32(N_SEC - 1), values)
    return values.astype(jnp.int32)


def plant(values, own_key, smallest, high):
    dims = values.shape
    index_at = [jax.random.randint(jax.random.fold_in(own_key, axis), (), 0, dims[axis]) for axis in range(len(dims))]
    values = values.at[tuple(index_at)].set(smallest)
    longest = dims.index(max(dims))
    index_at[longest] = (index_at[longest] + 1) % dims[longest]
    return values.at[tuple(index_at)].set(high)


def block_scale(own_key, dims, cuts, smallest, top_value):
    def one(axis_at, shards_of):
        heights = jax.random.uniform(jax.random.fold_in(jax.random.fold_in(own_key, 6), axis_at), (shards_of,), jnp.float32, smallest / len(cuts), top_value / len(cuts))
        return jnp.repeat(jnp.exp(heights), dims[axis_at] // shards_of).reshape((-1,) + (1,) * (len(dims) - axis_at - 1))

    gain = one(*cuts[0])
    for cut in cuts[1:]:
        gain = gain * one(*cut)
    return gain


def normal_values(rng, extent, width, bound, cuts=(), kind=jnp.bfloat16):
    entries = jax.random.normal(rng, extent, jnp.float32) * width
    if len(cuts) > 0:
        entries = block_scale(rng, extent, cuts, -0.22, 0.18) * entries
    return jnp.clip(entries, min=-bound, max=bound).astype(kind)


def setup_inputs(seed: int = 0) -> dict:
    seeds = jax.random.split(jax.random.key(seed), 8)
    state = normal_values(seeds[0], (2, FIELDS, NQ, NT), 1.0, 6.0, ((0, 2), (2, 4), (3, 64)), jnp.float32)
    damping = jnp.clip(jnp.exp(math.log(1.0) - 2.3025851 * jax.random.uniform(seeds[1], (2, NQ, NT), jnp.float32) ** block_scale(seeds[1], (2, NQ, NT), ((0, 2), (1, 4), (2, 64)), -0.2, 0.2)), 0.1, 1.0)
    jac_axial = normal_values(seeds[2], (2, FIELDS, FIELDS), FIELDS ** -0.5, 2.5, ((0, 2),), jnp.float32)
    jac_angular = normal_values(seeds[3], (2, FIELDS, FIELDS), FIELDS ** -0.5, 2.5, ((0, 2),), jnp.float32)
    section_shift = draw_section_shift(jax.random.fold_in(seeds[7], 71), 0)
    donor_offset = plant(jax.random.randint(seeds[5], (NT,), 0, OFFSETS), jax.random.fold_in(seeds[5], 1), 0, OFFSETS - 1).astype(jnp.int32)
    match_weight = jnp.clip(jnp.exp(jax.random.uniform(seeds[6], (DONORS, NT), jnp.float32, math.log(0.1), math.log(1.0))), 0.1, 1.0)
    return dict(state=state, damping=damping, jac_axial=jac_axial, jac_angular=jac_angular, section_shift=section_shift, donor_offset=donor_offset, match_weight=match_weight)


time_step = 0.3
viscosity = 0.05


def stencil(padded, axis, count):
    def window(offset):
        return lax.slice_in_dim(padded, 2 + offset, 2 + offset + count, axis=axis)
    first = (8.0 * (window(1) - window(-1)) - (window(2) - window(-2))) / 12.0
    second = window(1) - 2.0 * window(0) + window(-1)
    return first, second


def apply_matrix(matrix, fields):
    results = []
    for target in range(5):
        total = matrix[target, 0] * fields[0]
        for source in range(1, 5):
            total = total + matrix[target, source] * fields[source]
        results.append(total)
    return jnp.stack(results)


def tendency(fields, q_padded, t_padded, axial, angular, damping):
    grad_q, lap_q = stencil(q_padded, 1, fields.shape[1])
    grad_t, lap_t = stencil(t_padded, 2, fields.shape[2])
    flux = apply_matrix(axial, grad_q) + apply_matrix(angular, grad_t)
    return viscosity * (lap_q + lap_t) - flux - damping * fields


def ghosts(other, shift, direction_sign, donor_offset, weights):
    layers = jnp.stack([other[:, NQ - 1, :], other[:, NQ - 2, :]], axis=1)
    angle = jnp.arange(NT, dtype=jnp.int32)
    total = jnp.zeros(layers.shape, jnp.float32)
    for donor in range(DONORS):
        index = ((angle + direction_sign * shift * CT + donor_offset + donor) % NT).astype(jnp.int32)
        total = total + weights[donor] * jnp.take(layers, index, axis=2)
    return total


def reference(state, damping, jac_axial, jac_angular, section_shift, donor_offset, match_weight):
    weights = match_weight / jnp.sum(match_weight, axis=0)
    axial = 0.5 * (jac_axial + jnp.swapaxes(jac_axial, 1, 2))
    angular = 0.5 * (jac_angular + jnp.swapaxes(jac_angular, 1, 2))

    def rhs(current, shift):
        results = []
        for blade in range(2):
            fields = current[blade]
            edge = ghosts(current[1 - blade], shift, 1 - 2 * blade, donor_offset, weights)
            q_padded = jnp.concatenate([jnp.zeros((5, 2, NT), jnp.float32), fields, edge], axis=1)
            t_padded = jnp.concatenate([fields[:, :, NT - 2:], fields, fields[:, :, :2]], axis=2)
            results.append(tendency(fields, q_padded, t_padded, axial[blade], angular[blade], damping[blade]))
        return jnp.stack(results)

    first = state + time_step * rhs(state, section_shift[0])
    second = 0.75 * state + 0.25 * (first + time_step * rhs(first, section_shift[1]))
    return state / 3.0 + (2.0 / 3.0) * (second + time_step * rhs(second, section_shift[2]))
```

```python
import functools

import jax
import jax.numpy as jnp
from jax import lax
from jax.experimental import pallas as pl
from jax.experimental.pallas import tpu as pltpu
from jax.sharding import PartitionSpec as P

DONORS = 4
FIELDS = 5
STEP = 0.3
VISCOSITY = 0.05
AXES = ("row", "grp", "sec")

EDGE = 8
WIDE = 24
PACK = 16
REACH = 6

VMEM = pl.BlockSpec(memory_space=pltpu.VMEM)
SMEM = pl.BlockSpec(memory_space=pltpu.SMEM)


def lanes(shape):
    return lax.broadcasted_iota(jnp.int32, shape, len(shape) - 1)


def scaled_matrices(axial_ref, angular_ref):
    scale = STEP * 2.0 / 3.0 * 0.5

    def one(ref):
        rows = [[None] * FIELDS for _ in range(FIELDS)]
        for i in range(FIELDS):
            for j in range(i, FIELDS):
                rows[i][j] = rows[j][i] = scale * (ref[0, i, j] + ref[0, j, i])
        return rows

    return one(axial_ref), one(angular_ref)


def increments(load, damping, matrices, width):
    axial, angular = matrices
    centre, grad_q, grad_t, lap = [], [], [], []
    for f in range(FIELDS):
        x = load(f, 0)
        down1, up1 = load(f, -1)[:, :width], load(f, 1)[:, :width]
        down2, up2 = load(f, -2)[:, :width], load(f, 2)[:, :width]
        span = x.shape[1]
        right1 = pltpu.roll(x, span - 1, 1)[:, :width]
        left1 = pltpu.roll(x, 1, 1)[:, :width]
        right2 = pltpu.roll(x, span - 2, 1)[:, :width]
        left2 = pltpu.roll(x, 2, 1)[:, :width]
        x = x[:, :width]
        grad_q.append((up1 - down1) - 0.125 * (up2 - down2))
        grad_t.append((right1 - left1) - 0.125 * (right2 - left2))
        lap.append((up1 + down1) + (right1 + left1))
        centre.append(x)
    decay = STEP * damping + 4.0 * STEP * VISCOSITY
    results = []
    for i in range(FIELDS):
        flux = axial[i][0] * grad_q[0] + angular[i][0] * grad_t[0]
        for j in range(1, FIELDS):
            flux = flux + (axial[i][j] * grad_q[j] + angular[i][j] * grad_t[j])
        results.append((STEP * VISCOSITY) * lap[i] - flux - decay * centre[i])
    return centre, results


def ghost_layers(layers, coeff_ref):
    total = coeff_ref[0:1, :] * layers
    for distance in range(1, 2 * DONORS - 1):
        moved = pltpu.roll(layers, 256 - distance, 1)
        total = total + coeff_ref[distance : distance + 1, :] * moved
    return total


def pack_kernel(state_ref, damping_ref, first_ref, second_ref):
    even = lax.axis_index("sec") % 2 == 0
    group = lanes((PACK, 128)) // EDGE
    for a in range(FIELDS + 1):
        low = high = jnp.zeros((PACK, 128), jnp.float32)
        for j in range(128 // EDGE):
            rows = pl.ds(j * PACK, PACK)
            x = state_ref[0, a, rows, :] if a < FIELDS else damping_ref[0, rows, :]
            low = jnp.where(group == j, pltpu.roll(x, EDGE * j, 1) if j else x, low)
            shift = (EDGE * j + EDGE) % 128
            high = jnp.where(group == j, pltpu.roll(x, shift, 1) if shift else x, high)
        top = state_ref[0, a, 248:256, :] if a < FIELDS else damping_ref[0, 248:256, :]
        first_ref[a, 0:PACK, :] = jnp.where(even, high, low)
        second_ref[a, 0:PACK, :] = jnp.where(even, low, high)
        first_ref[a, PACK : PACK + 8, :] = top
        second_ref[a, PACK : PACK + 8, :] = top


def neighbours(even, first_ref, second_ref, a, rows):
    one = first_ref[jnp.where(even, 1, 0), a, rows, :]
    two = second_ref[jnp.where(even, 0, 1), a, rows, :]
    return jnp.where(even, one, two), jnp.where(even, two, one)


def edge_kernel(
    first_ref, second_ref, state_ref, damping_ref, weight_ref, offset_ref,
    rows_b_ref, rows_c_ref, send_ref, strip_ref, coeff_ref,
):
    sec = lax.axis_index("sec")
    grp = lax.axis_index("grp")
    even = sec % 2 == 0
    lane = lanes((8, 128))
    for a in range(FIELDS + 1):
        here = (lambda r: state_ref[0, a, r, :]) if a < FIELDS else (lambda r: damping_ref[0, r, :])
        right, left = neighbours(even, first_ref, second_ref, a, slice(PACK, PACK + 8))
        side = jnp.where(lane < WIDE, right, jnp.where(lane >= 128 - EDGE, left, 0.0))
        high = jnp.concatenate([here(slice(248, 256)), side], axis=1)
        right, left = neighbours(even, first_ref, second_ref, a, slice(0, 8))
        left = pltpu.roll(left, 128 - EDGE, 1)
        side = jnp.where(lane < EDGE, right, jnp.where(lane >= 128 - EDGE, left, 0.0))
        low = jnp.concatenate([here(slice(0, 8)), side], axis=1)
        rows_b_ref[a] = jnp.where(grp % 2 == 0, high, low)
        rows_c_ref[a] = jnp.where(grp == 2, low, high)
        strip_ref[a] = high
        if a < FIELDS:
            send_ref[2 * a : 2 * a + 1, :] = high[7:8, :]
            send_ref[2 * a + 1 : 2 * a + 2, :] = high[6:7, :]
    send_ref[10:16, :] = jnp.zeros((6, 256), jnp.float32)

    sectors = weight_ref.shape[1] // 128

    def window(ref, which):
        start = pl.multiple_of(((sec + which + sectors) % sectors) * 128, 128)
        return ref[:, pl.ds(start, 128)]

    def extended(ref):
        near, right, left = (window(ref, k) for k in (0, 1, -1))
        side = jnp.where(lanes(right.shape) < 64, right, left)
        return jnp.concatenate([near, side], axis=1)

    weight = extended(weight_ref)
    total = weight[0:1] + weight[1:2] + weight[2:3] + weight[3:4]
    weight = weight / total
    offset = extended(offset_ref)
    for distance in range(2 * DONORS - 1):
        coeff = jnp.zeros((1, 256), jnp.float32)
        for k in range(DONORS):
            coeff = coeff + jnp.where(offset == distance - k, weight[k : k + 1], 0.0)
        coeff_ref[distance : distance + 1, :] = coeff
    coeff_ref[7:8, :] = jnp.zeros((1, 256), jnp.float32)


def strip_kernel(
    stage, axial_ref, angular_ref, coeff_ref, got_ref, strip_ref, *refs,
):
    if stage == 0:
        now_ref = strip_ref
        out_ref, ghost_ref, send_ref, rows_ref = refs
    else:
        now_ref, out_ref, ghost_ref, send_ref, rows_ref = refs
    matrices = scaled_matrices(axial_ref, angular_ref)
    ghost = ghost_layers(got_ref[1 - lax.axis_index("row")], coeff_ref)
    ghost_ref[...] = ghost
    for f in range(FIELDS):
        rows_ref[f, 0:8, :] = jnp.zeros((8, 256), jnp.float32)
        rows_ref[f, 8:16, :] = now_ref[f]
        rows_ref[f, 16:18, :] = ghost[2 * f : 2 * f + 2, :]
        rows_ref[f, 18:24, :] = jnp.zeros((6, 256), jnp.float32)
    centre, more = increments(
        lambda f, k: rows_ref[f, 8 + k : 16 + k, :], strip_ref[FIELDS], matrices, 256
    )
    for f in range(FIELDS):
        new = centre[f] + more[f]
        if stage == 1:
            new = 0.75 * strip_ref[f] + 0.25 * new
        out_ref[f] = new
        send_ref[2 * f : 2 * f + 1, :] = new[7:8, :]
        send_ref[2 * f + 1 : 2 * f + 2, :] = new[6:7, :]
    send_ref[10:16, :] = jnp.zeros((6, 256), jnp.float32)


def step_kernel(
    axial_ref, angular_ref, coeff_ref, got_ref, ghost0_ref, ghost1_ref,
    first_ref, second_ref, rows_b_ref, rows_c_ref, state_ref, damping_ref,
    out_ref, whole_ref, x_ref, y_ref, z_ref, d_ref,
):
    sec = lax.axis_index("sec")
    grp = lax.axis_index("grp")
    even = sec % 2 == 0
    lane = lanes((PACK, 128))
    matrices = scaled_matrices(axial_ref, angular_ref)
    ghost2 = ghost_layers(got_ref[1 - lax.axis_index("row")], coeff_ref)

    for a in range(FIELDS + 1):
        source = state_ref.at[0, a] if a < FIELDS else damping_ref.at[0]
        right, left = neighbours(even, first_ref, second_ref, a, slice(0, PACK))
        for j in range(128 // EDGE):
            r = pltpu.roll(right, 128 - EDGE * j, 1) if j else right
            l = pltpu.roll(left, (128 - EDGE - EDGE * j) % 128, 1) if j < 15 else left
            side = jnp.where(lane < EDGE, r, jnp.where(lane >= 128 - EDGE, l, 0.0))
            whole_ref[a, 0, 8 + PACK * j : 8 + PACK * (j + 1), :] = source[pl.ds(PACK * j, PACK), :]
            whole_ref[a, 1, 8 + PACK * j : 8 + PACK * (j + 1), :] = side
        rows_b, rows_c = rows_b_ref[a], rows_c_ref[a]
        low = jnp.where(grp % 2 == 1, rows_b, rows_c)
        low = jnp.where(grp == 0, 0.0, low)
        high = jnp.where(grp % 2 == 0, rows_b, rows_c)
        high = jnp.where(grp == 3, 0.0, high)
        for h in range(2):
            whole_ref[a, h, 0:8, :] = low[:, 128 * h : 128 * (h + 1)]
            whole_ref[a, h, 264:272, :] = high[:, 128 * h : 128 * (h + 1)]
        for i in range(-REACH, 32 + REACH):
            for h in range(2):
                rows = whole_ref[a, h, pl.ds(8 + i, 8, stride=32), :]
                if a < FIELDS:
                    x_ref[a, i + REACH, :, 128 * h : 128 * (h + 1)] = rows
                else:
                    d_ref[i + REACH, :, 128 * h : 128 * (h + 1)] = rows

    def outer(ref, ghost, reach):
        @pl.when(grp == 3)
        def _():
            for f in range(FIELDS):
                for m in range(2):
                    ref[f, REACH + 32 + m, 7:8, :] = ghost[2 * f + m : 2 * f + m + 1, :]

        @pl.when(grp == 0)
        def _():
            for f in range(FIELDS):
                for i in range(-reach, 0):
                    ref[f, REACH + i, 0:1, :] = jnp.zeros((1, 256), jnp.float32)

    def block(ref, i, width):
        return increments(lambda f, k: ref[f, i + k], d_ref[i][:, :width], matrices, width)

    outer(x_ref, ghost0_ref[...], 0)

    @pl.loop(REACH - 4, REACH + 36)
    def _(i):
        centre, more = block(x_ref, i, 256)
        for f in range(FIELDS):
            y_ref[f, i] = centre[f] + more[f]

    outer(y_ref, ghost1_ref[...], 4)

    @pl.loop(REACH - 2, REACH + 34)
    def _(i):
        centre, more = block(y_ref, i, 256)
        for f in range(FIELDS):
            z_ref[f, i] = 0.75 * x_ref[f, i] + 0.25 * (centre[f] + more[f])

    outer(z_ref, ghost2, 2)

    @pl.loop(REACH, REACH + 32)
    def _(i):
        centre, more = block(z_ref, i, 128)
        for f in range(FIELDS):
            new = x_ref[f, i][:, :128] / 3.0 + (2.0 / 3.0) * (centre[f] + more[f])
            out_ref[0, f, pl.ds(i - REACH, 8, stride=32), :] = new


def call(kernel, in_specs, out_shapes, scratch=()):
    return pl.pallas_call(
        kernel,
        in_specs=in_specs,
        out_specs=[VMEM] * len(out_shapes),
        out_shape=[jax.ShapeDtypeStruct(s, jnp.float32) for s in out_shapes],
        scratch_shapes=list(scratch),
        compiler_params=pltpu.CompilerParams(vmem_limit_bytes=48 * 1024 * 1024),
    )


def solution(mesh):
    groups, sectors = mesh.shape["grp"], mesh.shape["sec"]

    def device(row, grp, sec):
        return (row * groups + grp) * sectors + sec % sectors

    everywhere = [(r, g) for r in range(2) for g in range(groups)]
    cores = [
        [device(r, g, c), device(r, g, c + 1)] for r, g in everywhere for c in range(0, sectors, 2)
    ]
    chips = [
        [device(r, g, c), device(r, g, c + 1)] for r, g in everywhere for c in range(1, sectors, 2)
    ]

    def swap(lows):
        pairs = []
        for r in range(2):
            for g in lows:
                for c in range(sectors):
                    one, two = device(r, g, c), device(r, g + 1, c)
                    pairs += [(one, two), (two, one)]
        return pairs

    def across(shift):
        pairs = [[device(0, groups - 1, c), device(1, groups - 1, c + shift)] for c in range(sectors)]
        return pairs + [
            [device(r, g, c), device(r, g, c + 1)]
            for r, g in everywhere
            if g < groups - 1
            for c in range(0, sectors, 2)
        ]

    def gather(x, members):
        return lax.all_gather(x, AXES, axis_index_groups=members)

    def moved(got, direction):
        row, even = lax.axis_index("row"), lax.axis_index("sec") % 2 == 0
        mine = jnp.where(row == 0, got[1], got[0])
        one, two = gather(mine, cores), gather(mine, chips)
        ahead = jnp.where(even, one[1], two[1])
        behind = jnp.where(even, two[0], one[0])
        result = jnp.where((row == 0) == (direction > 0), ahead, behind)
        return jnp.stack([result, result])

    def branch(shift):
        if shift == sectors - 2:
            return lambda x: moved(gather(x, across(sectors - 1)), -1)
        if shift % 2 == 1 and shift != sectors - 1:
            return lambda x: moved(gather(x, across(shift - 1)), 1)
        return lambda x: gather(x, across(shift))

    branches = [branch(s) for s in range(sectors)]

    def exchange(x, shift):
        return lax.switch(shift, branches, x)

    def shards(state, damping, jac_axial, jac_angular, section_shift, donor_offset, match_weight):
        arrays = FIELDS + 1
        first, second = call(pack_kernel, [VMEM] * 2, [(arrays, PACK + 8, 128)] * 2)(state, damping)
        first = gather(first, cores)
        second = gather(second, chips)
        rows_b, rows_c, send, strip, coeff = call(
            edge_kernel, [VMEM] * 6, [(arrays, 8, 256)] * 2 + [(16, 256), (arrays, 8, 256), (8, 256)]
        )(first, second, state, damping, match_weight, donor_offset[None, :])
        rows_b = lax.ppermute(rows_b, AXES, swap((0, 2)))
        rows_c = lax.ppermute(rows_c, AXES, swap((1,)))
        strip_out = [(FIELDS, 8, 256), (16, 256), (16, 256)]
        rows = [pltpu.VMEM((FIELDS, 24, 256), jnp.float32)]

        got = exchange(send, section_shift[0])
        strip1, ghost0, send = call(
            functools.partial(strip_kernel, 0), [SMEM] * 2 + [VMEM] * 3, strip_out, rows
        )(jac_axial, jac_angular, coeff, got, strip)
        got = exchange(send, section_shift[1])
        _, ghost1, send = call(
            functools.partial(strip_kernel, 1), [SMEM] * 2 + [VMEM] * 4, strip_out, rows
        )(jac_axial, jac_angular, coeff, got, strip, strip1)
        got = exchange(send, section_shift[2])
        depth = 32 + 2 * REACH
        fields = pltpu.VMEM((FIELDS, depth, 8, 256), jnp.float32)
        (out,) = call(
            step_kernel,
            [SMEM] * 2 + [VMEM] * 10,
            [(1, FIELDS, 256, 128)],
            [pltpu.VMEM((arrays, 2, 272, 128), jnp.float32)]
            + [fields] * 3
            + [pltpu.VMEM((depth, 8, 256), jnp.float32)],
        )(jac_axial, jac_angular, coeff, got, ghost0, ghost1, first, second, rows_b, rows_c, state, damping)
        return out

    return jax.shard_map(
        shards,
        mesh=mesh,
        in_specs=(
            P("row", None, "grp", "sec"),
            P("row", "grp", "sec"),
            P("row", None, None),
            P("row", None, None),
            P(),
            P(),
            P(),
        ),
        out_specs=P("row", None, "grp", "sec"),
        check_vma=False,
    )
```

```python
import functools

import jax
import jax.numpy as jnp
from jax import lax
from jax.experimental import pallas as pl
from jax.experimental.pallas import tpu as pltpu
from jax.sharding import PartitionSpec as P

DONORS = 4
FIELDS = 5
STEP = 0.3
VISCOSITY = 0.05
AXES = ("row", "grp", "sec")

EDGE = 8
WIDE = 24
SECTORS = 64
ROUTE = (4,)
UNROLL = 4
REACH = 6

VMEM = pl.BlockSpec(memory_space=pltpu.VMEM)
ANY = pl.BlockSpec(memory_space=pl.ANY)
HBM = pl.BlockSpec(memory_space=pltpu.HBM)
SMEM = pl.BlockSpec(memory_space=pltpu.SMEM)


def lanes(shape):
    return lax.broadcasted_iota(jnp.int32, shape, len(shape) - 1)


def unique(i, j):
    i, j = min(i, j), max(i, j)
    return i * FIELDS - i * (i - 1) // 2 + j - i


ENTRIES = FIELDS * (FIELDS + 1) // 2


def advance(x, up1, down1, up2, down2, right1, left1, right2, left2, damping, matrices_ref):
    fields = range(FIELDS)
    grad_q = [(up1[f] - down1[f]) - 0.125 * (up2[f] - down2[f]) for f in fields]
    grad_t = [(right1[f] - left1[f]) - 0.125 * (right2[f] - left2[f]) for f in fields]
    keep = (1.0 - 4.0 * STEP * VISCOSITY) - STEP * damping
    results = []
    for i in fields:
        flux = None
        for j in fields:
            term = matrices_ref[unique(i, j)] * grad_q[j] + matrices_ref[ENTRIES + unique(i, j)] * grad_t[j]
            flux = term if flux is None else flux + term
        lap = (up1[i] + down1[i]) + (right1[i] + left1[i])
        results.append(keep * x[i] + ((STEP * VISCOSITY) * lap - flux))
    return results


def turned(near, side, lane):
    result = []
    for shift in (127, 1, 126, 2):
        one, two = pltpu.roll(near, shift, 1), pltpu.roll(side, shift, 1)
        inner = lane < shift if shift > 64 else lane >= shift
        result.append((jnp.where(inner, one, two), jnp.where(inner, two, one)))
    return result


def both(load, damping, matrices_ref, sides):
    fields = range(FIELDS)
    lane = lanes((8, 128))
    turns = [turned(load(f, 0, 0), load(f, 0, 1), lane) for f in fields]
    return [
        advance(
            [load(f, 0, h) for f in fields],
            *([load(f, k, h) for f in fields] for k in (1, -1, 2, -2)),
            *([turns[f][n][h] for f in fields] for n in range(4)),
            damping(h),
            matrices_ref,
        )
        for h in range(sides)
    ]


def ghost_layers(layers, coeff_ref):
    total = coeff_ref[0:1, :] * layers
    for distance in range(1, 2 * DONORS - 1):
        moved = pltpu.roll(layers, 256 - distance, 1)
        total = total + coeff_ref[distance : distance + 1, :] * moved
    return total


def spot(a):
    return 64 * (a // 4), EDGE * (a % 4)


def pack_kernel(
    state_ref, damping_ref, axial_ref, angular_ref, shift_ref,
    first_ref, second_ref, held_ref, own_ref, matrices_ref, route_ref, jac_ref, three_ref, sems,
):
    count = FIELDS + 1
    copies = []
    for a in range(count):
        source = state_ref.at[0, a] if a < FIELDS else damping_ref.at[0]
        copies.append(pltpu.make_async_copy(source, held_ref.at[a], sems.at[a]))
    for n, ref in enumerate((axial_ref, angular_ref)):
        copies.append(pltpu.make_async_copy(ref, jac_ref.at[n], sems.at[count + n]))
    copies.append(pltpu.make_async_copy(shift_ref, three_ref, sems.at[count + 2]))
    for copy in reversed(copies):
        copy.start()
    even = lax.axis_index("sec") % 2 == 0
    lane = lanes((8, 128))

    copies[count + 2].wait()
    half, last = SECTORS // 2, SECTORS - 1
    s0, s1, s2 = three_ref[0], three_ref[1], three_ref[2]
    at_half = jnp.where(s0 == half, 0, jnp.where(s1 == half, 1, 2))
    at_last = jnp.where(s0 == last, 0, jnp.where(s1 == last, 1, 2))
    free = 3 - at_half - at_last
    shift = jnp.where(free == 0, s0, jnp.where(free == 1, s1, s2))
    odd = shift & 1
    route_ref[0] = 2 * at_half + at_last - jnp.where(at_last > at_half, 1, 0)
    route_ref[1] = jnp.where(shift >= last - 1, half - 1, lax.shift_right_logical(shift, 1))
    route_ref[2] = jnp.where(odd == 0, jnp.where(shift == last - 1, 0, 1), jnp.where(shift == last, 1, 0))
    route_ref[3] = jnp.where(shift == last - 1, 1, 0)

    scale = STEP * 2.0 / 3.0 * 0.5
    for n in range(2):
        copies[count + n].wait()
        for i in range(FIELDS):
            for j in range(i, FIELDS):
                entry = scale * (jac_ref[n, i, :, j : j + 1] + jac_ref[n, j, :, i : i + 1])
                matrices_ref[ENTRIES * n + unique(i, j)] = jnp.broadcast_to(entry, (8, 128))

    for b in range(2):
        arrays = range(4 * b, min(4 * b + 4, count))
        for a in arrays:
            copies[a].wait()
        for i in range(8):
            low = high = jnp.zeros((8, 128), jnp.float32)
            for a in arrays:
                for k in range(4):
                    x = held_ref[a, pl.ds(8 * k + i, 8, stride=32), :]
                    place = 32 * k + spot(a)[1]
                    here = (lane >= place) & (lane < place + EDGE)
                    low = jnp.where(here, pltpu.roll(x, place, 1) if place else x, low)
                    shift = (place + EDGE) % 128
                    high = jnp.where(here, pltpu.roll(x, shift, 1) if shift else x, high)
            rows = slice(64 * b + 8 * i, 64 * b + 8 * i + 8)
            own_ref[0, rows, :] = low
            own_ref[1, rows, :] = high
            first_ref[rows, :] = jnp.where(even, high, low)
            second_ref[rows, :] = jnp.where(even, low, high)
        tops = jnp.zeros((8, 128), jnp.float32)
        for a in arrays:
            top, place = held_ref[a, 248:256, :], 32 * (a % 4)
            wide = (lane >= place) & (lane < place + WIDE)
            tops = jnp.where(wide, pltpu.roll(top, place, 1) if place else top, tops)
            narrow = (lane >= place + WIDE) & (lane < place + 32)
            shift = (place + 32) % 128
            tops = jnp.where(narrow, pltpu.roll(top, shift, 1) if shift else top, tops)
        first_ref[128 + 8 * b : 136 + 8 * b, :] = tops
        second_ref[128 + 8 * b : 136 + 8 * b, :] = tops


def neighbours(even, first_ref, second_ref, rows):
    one = first_ref[jnp.where(even, 1, 0), rows, :]
    two = second_ref[jnp.where(even, 0, 1), rows, :]
    return jnp.where(even, one, two), jnp.where(even, two, one)


def rotate(x, shift):
    shift %= 128
    return pltpu.roll(x, shift, 1) if shift else x


def edge_kernel(
    first_ref, second_ref, held_ref, weight_ref, offset_ref,
    rows_b_ref, rows_c_ref, send_ref, strip_ref, coeff_ref,
):
    sec = lax.axis_index("sec")
    grp = lax.axis_index("grp")
    even = sec % 2 == 0
    lane = lanes((8, 128))

    def side(right, left, count):
        return jnp.where(lane < count, right, jnp.where(lane >= 128 - EDGE, left, 0.0))

    for a in range(FIELDS + 1):
        start, place = spot(a)
        right, left = neighbours(even, first_ref, second_ref, slice(128 + 8 * (a // 4), 136 + 8 * (a // 4)))
        top = 32 * (a % 4)
        high = jnp.concatenate(
            [held_ref[a, 248:256, :], side(rotate(right, -top), rotate(left, 96 - top), WIDE)], axis=1
        )
        right, left = neighbours(even, first_ref, second_ref, pl.ds(start, 8, stride=8))
        low = jnp.concatenate(
            [held_ref[a, 0:8, :], side(rotate(right, -place), rotate(left, -EDGE - place), EDGE)], axis=1
        )
        right, left = neighbours(even, first_ref, second_ref, pl.ds(start + 7, 8, stride=8))
        place = place + 64
        strip_ref[a, 0:8, 0:128] = held_ref[a, 240:248, :]
        strip_ref[a, 0:8, 128:256] = side(rotate(right, -place), rotate(left, -EDGE - place), EDGE)
        strip_ref[a, 8:16, :] = high
        rows_b_ref[a] = jnp.where(grp % 2 == 0, high, low)
        rows_c_ref[a] = jnp.where(grp == 2, low, high)
        if a < FIELDS:
            send_ref[2 * a : 2 * a + 1, :] = high[7:8, :]
            send_ref[2 * a + 1 : 2 * a + 2, :] = high[6:7, :]
    send_ref[10:16, :] = jnp.zeros((6, 256), jnp.float32)

    sectors = weight_ref.shape[1] // 128

    def window(ref, which):
        start = pl.multiple_of(((sec + which + sectors) % sectors) * 128, 128)
        return ref[:, pl.ds(start, 128)]

    def extended(ref):
        near, right, left = (window(ref, k) for k in (0, 1, -1))
        return jnp.concatenate([near, jnp.where(lanes(right.shape) < 64, right, left)], axis=1)

    weight = extended(weight_ref)
    total = weight[0:1] + weight[1:2] + weight[2:3] + weight[3:4]
    weight = weight / total
    offset = extended(offset_ref)
    for distance in range(2 * DONORS - 1):
        coeff = jnp.zeros((1, 256), jnp.float32)
        for k in range(DONORS):
            coeff = coeff + jnp.where(offset == distance - k, weight[k : k + 1], 0.0)
        coeff_ref[distance : distance + 1, :] = coeff
    coeff_ref[7:8, :] = jnp.zeros((1, 256), jnp.float32)


def layers_of(got_ref):
    return got_ref[...] if len(got_ref.shape) == 2 else got_ref[1 - lax.axis_index("row")]


def strip_stage(now_ref, got_ref, strip_ref, coeff_ref, matrices_ref, rows_ref, blocks, sides):
    ghost = ghost_layers(layers_of(got_ref), coeff_ref)
    for f in range(FIELDS):
        rows_ref[f, 0:8, :] = jnp.zeros((8, 256), jnp.float32)
        rows_ref[f, 8:24, :] = now_ref[f]
        rows_ref[f, 24:26, :] = ghost[2 * f : 2 * f + 2, :]
        rows_ref[f, 26:32, :] = jnp.zeros((6, 256), jnp.float32)

    def halves(h):
        return slice(128 * h, 128 * (h + 1))

    return [
        both(
            lambda f, k, h: rows_ref[f, 8 + 8 * b + k : 16 + 8 * b + k, halves(h)],
            lambda h: strip_ref[FIELDS, 8 * b : 8 * b + 8, halves(h)],
            matrices_ref,
            sides,
        )
        for b in blocks
    ]


def strip_kernel(stage, matrices_ref, coeff_ref, got_ref, strip_ref, *refs):
    now_ref, out_ref, send_ref, rows_ref = refs if stage else (strip_ref, *refs)
    new = strip_stage(now_ref, got_ref, strip_ref, coeff_ref, matrices_ref, rows_ref, (0, 1), 2)
    for b in range(2):
        for h in range(2):
            for f in range(FIELDS):
                place = f, slice(8 * b, 8 * b + 8), slice(128 * h, 128 * h + 128)
                value = new[b][h][f]
                if stage:
                    value = 0.75 * strip_ref[place] + 0.25 * value
                out_ref[place] = value
                if b:
                    send_ref[2 * f : 2 * f + 1, place[2]] = value[7:8, :]
                    send_ref[2 * f + 1 : 2 * f + 2, place[2]] = value[6:7, :]
    send_ref[10:16, :] = jnp.zeros((6, 256), jnp.float32)


def last_kernel(matrices_ref, coeff_ref, got_ref, strip_ref, now_ref, _, out_ref, rows_ref, new_ref, sem):
    ((new,),) = strip_stage(now_ref, got_ref, strip_ref, coeff_ref, matrices_ref, rows_ref, (1,), 1)
    for f in range(FIELDS):
        new_ref[f] = strip_ref[f, 8:16, 0:128] / 3.0 + (2.0 / 3.0) * new[f]

    @pl.when(lax.axis_index("grp") == 3)
    def _():
        copy = pltpu.make_async_copy(new_ref, out_ref.at[0, :, 248:256, :], sem)
        copy.start()
        copy.wait()


def block_kernel(
    matrices_ref, first_ref, second_ref, own_ref, rows_b_ref, rows_c_ref, held_ref,
    out_ref, x_ref, y_ref, z_ref, d_ref, gx_ref, gy_ref, gz_ref, ge_ref, gd_ref,
):
    sec = lax.axis_index("sec")
    grp = lax.axis_index("grp")
    even = sec % 2 == 0
    lane = lanes((8, 128))
    part = lane % 32
    row = lax.broadcasted_iota(jnp.int32, (8, 128), 0)

    def choose(far_left, own_left, own_right, far_right):
        return jnp.where(
            part < 16, jnp.where(part < 8, far_left, own_left), jnp.where(part < 24, own_right, far_right)
        )

    for a in range(FIELDS + 1):
        near = x_ref.at[a] if a < FIELDS else d_ref
        side = gx_ref.at[a] if a < FIELDS else gd_ref
        rows_b, rows_c = rows_b_ref[a], rows_c_ref[a]
        low = jnp.where(grp == 0, 0.0, jnp.where(grp % 2 == 1, rows_b, rows_c))
        high = jnp.where(grp == 3, 0.0, jnp.where(grp % 2 == 0, rows_b, rows_c))
        for i in range(32):
            near[REACH + i] = held_ref[a, pl.ds(i, 8, stride=32), :]
        for i in range(REACH):
            below = pltpu.roll(near[REACH + 32 - REACH + i], 1, 0)
            near[i] = jnp.where(row == 0, low[8 - REACH + i : 9 - REACH + i, 0:128], below)
            above = pltpu.roll(near[REACH + i], 7, 0)
            near[REACH + 32 + i] = jnp.where(row == 7, high[i : i + 1, 0:128], above)
        start, place = spot(a)
        for i in range(8):
            rows = slice(start + 8 * i, start + 8 * i + 8)
            right, left = neighbours(even, first_ref, second_ref, rows)
            side[REACH + i] = choose(
                rotate(left, -place),
                rotate(own_ref[0, rows, :], 8 - place),
                rotate(own_ref[1, rows, :], 16 - place),
                rotate(right, 24 - place),
            )
        low, high = (
            choose(rotate(h[:, 128:], 8), rotate(h[:, :128], 8), rotate(h[:, :128], 24), rotate(h[:, 128:], 24))
            for h in (low, high)
        )
        high = pltpu.roll(high, 96, 1)
        for i in range(REACH):
            below = pltpu.roll(side[REACH + 8 - REACH + i], 32, 1)
            below = jnp.where(lane < 32, pltpu.roll(below, 1, 0), below)
            edge = (row == 0) & (lane < 32)
            side[i] = jnp.where(edge, low[8 - REACH + i : 9 - REACH + i, :], below)
            above = pltpu.roll(side[REACH + i], 96, 1)
            above = jnp.where(lane >= 96, pltpu.roll(above, 7, 0), above)
            edge = (row == 7) & (lane >= 96)
            side[REACH + 8 + i] = jnp.where(edge, high[i : i + 1, :], above)

    def nothing_before(near, side, reach):
        @pl.when(grp == 0)
        def _():
            for f in range(FIELDS):
                for i in range(REACH - reach, REACH):
                    near[f, i, 0:1, :] = jnp.zeros((1, 128), jnp.float32)
                    side[f, i, 0:1, 0:32] = jnp.zeros((1, 32), jnp.float32)

    fields = range(FIELDS)

    def axial(ref, i):
        return ([ref[f, i + k] for f in fields] for k in (0, 1, -1, 2, -2))

    def turns(x):
        return ([pltpu.roll(v, shift, 1) for v in x] for shift in (127, 1, 126, 2))

    def near_stage(near, side_new, first, last, store):
        @pl.loop(REACH + first, REACH + last, unroll=UNROLL)
        def _(i):
            k = jnp.clip(lax.shift_right_arithmetic(i - REACH, 3), 0, 3)
            x, *others = axial(near, i)
            new = advance(x, *others, *turns(x), d_ref[i], matrices_ref)
            for f in fields:
                beside = side_new[f, i - 8 * k]
                low = pltpu.roll(beside, (120 - 32 * k) & 127, 1)
                high = pltpu.roll(beside, (104 - 32 * k) & 127, 1)
                new[f] = jnp.where(lane < 2, low, jnp.where(lane >= 126, high, new[f]))
            store(i, new)

    def side_stage(side, first, last, store):
        @pl.loop(REACH + first, REACH + last, unroll=2)
        def _(i):
            x, *others = axial(side, i)
            store(i, advance(x, *others, *turns(x), gd_ref[i], matrices_ref))

    def plain(ref):
        def store(i, new):
            for f in fields:
                ref[f, i] = new[f]

        return store

    def blended(old, weights, put):
        def store(i, new):
            for f in fields:
                put(f, i, weights[0] * old[f, i] + weights[1] * new[f])

        return store

    def into(ref):
        def put(f, i, value):
            ref[f, i] = value

        return put

    def out(f, i, value):
        out_ref[0, f, pl.ds(i - REACH, 8, stride=32), :] = value

    side_stage(gx_ref, -4, 12, plain(gy_ref))
    near_stage(x_ref, gy_ref, -4, 36, plain(y_ref))
    nothing_before(y_ref, gy_ref, 4)
    side_stage(gy_ref, -2, 10, plain(ge_ref))
    near_stage(y_ref, ge_ref, -2, 34, blended(x_ref, (0.75, 0.25), into(z_ref)))
    for i in range(REACH - 2, REACH + 10):
        for f in fields:
            gz_ref[f, i] = 0.75 * gx_ref[f, i] + 0.25 * ge_ref[f, i]
    nothing_before(z_ref, gz_ref, 2)
    side_stage(gz_ref, 0, 8, plain(ge_ref))
    near_stage(z_ref, ge_ref, 0, 32, blended(x_ref, (1.0 / 3.0, 2.0 / 3.0), out))


def call(kernel, in_specs, out_shapes, scratch=(), out_specs=None, flops=0, vmem=40, **options):
    return pl.pallas_call(
        kernel,
        in_specs=in_specs,
        out_specs=out_specs or [SMEM if s == ROUTE else VMEM for s in out_shapes],
        out_shape=[jax.ShapeDtypeStruct(s, jnp.int32 if s == ROUTE else jnp.float32) for s in out_shapes],
        scratch_shapes=list(scratch),
        compiler_params=pltpu.CompilerParams(vmem_limit_bytes=vmem * 1024 * 1024),
        cost_estimate=pl.CostEstimate(flops=flops, bytes_accessed=flops // 10, transcendentals=0) if flops else None,
        **options,
    )


def solution(mesh):
    groups, sectors = mesh.shape["grp"], mesh.shape["sec"]

    def device(row, grp, sec):
        return (row * groups + grp) * sectors + sec % sectors

    everywhere = [(r, g) for r in range(2) for g in range(groups)]
    cores = [
        [device(r, g, c), device(r, g, c + 1)] for r, g in everywhere for c in range(0, sectors, 2)
    ]
    chips = [
        [device(r, g, c), device(r, g, c + 1)] for r, g in everywhere for c in range(1, sectors, 2)
    ]

    def swap(lows):
        pairs = []
        for r in range(2):
            for g in lows:
                for c in range(sectors):
                    one, two = device(r, g, c), device(r, g + 1, c)
                    pairs += [(one, two), (two, one)]
        return pairs

    def across(shift):
        pairs = [[device(0, groups - 1, c), device(1, groups - 1, c + shift)] for c in range(sectors)]
        return pairs + [
            [device(r, g, c), device(r, g, c + 1)]
            for r, g in everywhere
            if g < groups - 1
            for c in range(0, sectors, 2)
        ]

    def gather(x, members):
        return lax.all_gather(x, AXES, axis_index_groups=members)

    half = sectors // 2
    opposite = [pair for one, two in across(half)[:sectors] for pair in ((one, two), (two, one))]

    def branch(shift):
        if shift == half:
            return lambda x: jnp.stack([lax.ppermute(x, AXES, opposite)] * 2)
        return lambda x: gather(x, across(shift))

    branches = [branch(s) for s in range(0, sectors - 2, 2)] + [branch(sectors - 1)]

    def moved(got, back):
        row, even = lax.axis_index("row"), lax.axis_index("sec") % 2 == 0
        mine = jnp.where(row == 0, got[1], got[0])
        one, two = gather(mine, cores), gather(mine, chips)
        ahead = jnp.where(even, one[1], two[1])
        behind = jnp.where(even, two[0], one[0])
        result = jnp.where((row == 0) != (back == 1), ahead, behind)
        return jnp.stack([result, result])

    def any_shift(send, nearest, exact, back):
        got = lax.switch(nearest, branches, send)
        return lax.switch(exact, [lambda got: moved(got, back), lambda got: got], got)

    arrays = FIELDS + 1
    strip_shape = (FIELDS, 16, 256)
    rows = pltpu.VMEM((FIELDS, 32, 256), jnp.float32)

    def variant(at_half, at_last):
        def run(
            nearest, exact, back, send,
            strip, coeff, matrices, first, second, own, rows_b, rows_c, held,
        ):
            rows_b = lax.ppermute(rows_b, AXES, swap((0, 2)))
            rows_c = lax.ppermute(rows_c, AXES, swap((1,)))
            now = ()
            for stage in range(3):
                if stage == at_half:
                    got = lax.ppermute(send, AXES, opposite)
                    near = (32 + 2 * REACH, 8, 128)
                    side = (8 + 2 * REACH, 8, 128)
                    shapes = [(FIELDS, *near)] * 3 + [near] + [(FIELDS, *side)] * 4 + [side]
                    send, rows_b = lax.optimization_barrier((send, rows_b))
                    (block,) = call(
                        block_kernel,
                        [VMEM] * 7,
                        [(1, FIELDS, 256, 128)],
                        [pltpu.VMEM(shape, jnp.float32) for shape in shapes],
                        flops=40_000_000,
                    )(matrices, first, second, own, rows_b, rows_c, held)
                    got, block = lax.optimization_barrier((got, block))
                elif stage == at_last:
                    got = gather(send, across(sectors - 1))
                else:
                    got = any_shift(send, nearest, exact, back)
                if stage < 2:
                    strip_now, send = call(
                        functools.partial(strip_kernel, stage),
                        [VMEM] * (4 + len(now)),
                        [strip_shape, (16, 256)],
                        [rows],
                    )(matrices, coeff, got, strip, *now)
                    now = (strip_now,)
            (out,) = call(
                last_kernel,
                [VMEM] * 5 + [ANY],
                [(1, FIELDS, 256, 128)],
                [rows, pltpu.VMEM((FIELDS, 8, 128), jnp.float32), pltpu.SemaphoreType.DMA],
                [ANY],
                input_output_aliases={5: 0},
            )(matrices, coeff, got, strip, *now, block)
            return out

        return run

    variants = [variant(i, j) for i in range(3) for j in range(3) if i != j]

    def shards(state, damping, jac_axial, jac_angular, section_shift, donor_offset, match_weight):
        first, second, held, own, matrices, route = call(
            pack_kernel,
            [HBM] * 5,
            [(144, 128)] * 2 + [(arrays, 256, 128), (2, 128, 128), (2 * ENTRIES, 8, 128), ROUTE],
            [
                pltpu.VMEM((2, FIELDS, 1, FIELDS), jnp.float32),
                pltpu.SMEM((3,), jnp.int32),
                pltpu.SemaphoreType.DMA((arrays + 3,)),
            ],
            vmem=58,
        )(state, damping, jnp.swapaxes(jac_axial, 0, 1), jnp.swapaxes(jac_angular, 0, 1), section_shift)
        which, nearest, exact, back = route[0], route[1], route[2], route[3]
        first = gather(first, cores)
        second = gather(second, chips)
        rows_b, rows_c, send, strip, coeff = call(
            edge_kernel,
            [VMEM] * 5,
            [(arrays, 8, 256)] * 2 + [(16, 256), (arrays, 16, 256), (8, 256)],
        )(first, second, held, match_weight, donor_offset[None, :])
        return lax.switch(
            which, variants, nearest, exact, back, send,
            strip, coeff, matrices, first, second, own, rows_b, rows_c, held,
        )

    return jax.shard_map(
        shards,
        mesh=mesh,
        in_specs=(
            P("row", None, "grp", "sec"),
            P("row", "grp", "sec"),
            P("row", None, None),
            P("row", None, None),
            P(),
            P(),
            P(),
        ),
        out_specs=P("row", None, "grp", "sec"),
        check_vma=False,
    )
```

```python
import functools

import jax
import jax.numpy as jnp
from jax import lax
from jax.experimental import pallas as pl
from jax.experimental.pallas import tpu as pltpu
from jax.sharding import PartitionSpec as P

DONORS = 4
FIELDS = 5
STEP = 0.3
VISCOSITY = 0.05
AXES = ("row", "grp", "sec")

EDGE = 8
WIDE = 24
SECTORS = 64
ROUTE = (1,)
UNROLL = 8
REACH = 6

VMEM = pl.BlockSpec(memory_space=pltpu.VMEM)
ANY = pl.BlockSpec(memory_space=pl.ANY)
HBM = pl.BlockSpec(memory_space=pltpu.HBM)
SMEM = pl.BlockSpec(memory_space=pltpu.SMEM)


def lanes(shape):
    return lax.broadcasted_iota(jnp.int32, shape, len(shape) - 1)


def unique(i, j):
    i, j = min(i, j), max(i, j)
    return i * FIELDS - i * (i - 1) // 2 + j - i


ENTRIES = FIELDS * (FIELDS + 1) // 2


def advance(x, up1, down1, up2, down2, right1, left1, right2, left2, damping, matrices_ref):
    fields = range(FIELDS)
    grad_q = [(up1[f] - down1[f]) - 0.125 * (up2[f] - down2[f]) for f in fields]
    grad_t = [(right1[f] - left1[f]) - 0.125 * (right2[f] - left2[f]) for f in fields]
    keep = (1.0 - 4.0 * STEP * VISCOSITY) - STEP * damping
    results = []
    for i in fields:
        flux = None
        for j in fields:
            term = matrices_ref[unique(i, j)] * grad_q[j] + matrices_ref[ENTRIES + unique(i, j)] * grad_t[j]
            flux = term if flux is None else flux + term
        lap = (up1[i] + down1[i]) + (right1[i] + left1[i])
        results.append(keep * x[i] + ((STEP * VISCOSITY) * lap - flux))
    return results


def turned(near, side, lane):
    result = []
    for shift in (127, 1, 126, 2):
        one, two = pltpu.roll(near, shift, 1), pltpu.roll(side, shift, 1)
        inner = lane < shift if shift > 64 else lane >= shift
        result.append((jnp.where(inner, one, two), jnp.where(inner, two, one)))
    return result


def both(load, damping, matrices_ref, sides):
    fields = range(FIELDS)
    lane = lanes((8, 128))
    turns = [turned(load(f, 0, 0), load(f, 0, 1), lane) for f in fields]
    return [
        advance(
            [load(f, 0, h) for f in fields],
            *([load(f, k, h) for f in fields] for k in (1, -1, 2, -2)),
            *([turns[f][n][h] for f in fields] for n in range(4)),
            damping(h),
            matrices_ref,
        )
        for h in range(sides)
    ]


def ghost_layers(layers, coeff_ref):
    total = coeff_ref[0:1, :] * layers
    for distance in range(1, 2 * DONORS - 1):
        moved = pltpu.roll(layers, 256 - distance, 1)
        total = total + coeff_ref[distance : distance + 1, :] * moved
    return total


def spot(a):
    return 64 * (a // 4), EDGE * (a % 4)


def pack_kernel(
    state_ref, damping_ref, axial_ref, angular_ref, shift_ref,
    first_ref, second_ref, held_ref, own_ref, matrices_ref,
    which_ref, nearest_ref, exact_ref, back_ref, jac_ref, three_ref, sems,
):
    count = FIELDS + 1
    copies = []
    for a in range(count):
        source = state_ref.at[0, a] if a < FIELDS else damping_ref.at[0]
        copies.append(pltpu.make_async_copy(source, held_ref.at[a], sems.at[a]))
    for n, ref in enumerate((axial_ref, angular_ref)):
        copies.append(pltpu.make_async_copy(ref, jac_ref.at[n], sems.at[count + n]))
    copies.append(pltpu.make_async_copy(shift_ref, three_ref, sems.at[count + 2]))
    for copy in reversed(copies):
        copy.start()
    even = lax.axis_index("sec") % 2 == 0
    lane = lanes((8, 128))

    copies[count + 2].wait()
    half, last = SECTORS // 2, SECTORS - 1
    s0, s1, s2 = three_ref[0], three_ref[1], three_ref[2]
    at_half = jnp.where(s0 == half, 0, jnp.where(s1 == half, 1, 2))
    at_last = jnp.where(s0 == last, 0, jnp.where(s1 == last, 1, 2))
    free = 3 - at_half - at_last
    shift = jnp.where(free == 0, s0, jnp.where(free == 1, s1, s2))
    odd = shift & 1
    which_ref[0] = 2 * at_half + at_last - jnp.where(at_last > at_half, 1, 0)
    nearest_ref[0] = jnp.where(shift >= last - 1, half - 1, lax.shift_right_logical(shift, 1))
    exact_ref[0] = jnp.where(odd == 0, jnp.where(shift == last - 1, 0, 1), jnp.where(shift == last, 1, 0))
    back_ref[0] = jnp.where(shift == last - 1, 1, 0)

    scale = STEP * 2.0 / 3.0 * 0.5
    for n in range(2):
        copies[count + n].wait()
        for i in range(FIELDS):
            for j in range(i, FIELDS):
                entry = scale * (jac_ref[n, i, :, j : j + 1] + jac_ref[n, j, :, i : i + 1])
                matrices_ref[ENTRIES * n + unique(i, j)] = jnp.broadcast_to(entry, (8, 128))

    for b in range(2):
        arrays = range(4 * b, min(4 * b + 4, count))
        for a in arrays:
            copies[a].wait()
        for i in range(8):
            low = high = jnp.zeros((8, 128), jnp.float32)
            for a in arrays:
                for k in range(4):
                    x = held_ref[a, pl.ds(8 * k + i, 8, stride=32), :]
                    place = 32 * k + spot(a)[1]
                    here = (lane >= place) & (lane < place + EDGE)
                    low = jnp.where(here, pltpu.roll(x, place, 1) if place else x, low)
                    shift = (place + EDGE) % 128
                    high = jnp.where(here, pltpu.roll(x, shift, 1) if shift else x, high)
            rows = slice(64 * b + 8 * i, 64 * b + 8 * i + 8)
            own_ref[0, rows, :] = low
            own_ref[1, rows, :] = high
            first_ref[rows, :] = jnp.where(even, high, low)
            second_ref[rows, :] = jnp.where(even, low, high)
        tops = jnp.zeros((8, 128), jnp.float32)
        for a in arrays:
            top, place = held_ref[a, 248:256, :], 32 * (a % 4)
            wide = (lane >= place) & (lane < place + WIDE)
            tops = jnp.where(wide, pltpu.roll(top, place, 1) if place else top, tops)
            narrow = (lane >= place + WIDE) & (lane < place + 32)
            shift = (place + 32) % 128
            tops = jnp.where(narrow, pltpu.roll(top, shift, 1) if shift else top, tops)
        first_ref[128 + 8 * b : 136 + 8 * b, :] = tops
        second_ref[128 + 8 * b : 136 + 8 * b, :] = tops


def neighbours(even, first_ref, second_ref, rows):
    one = first_ref[jnp.where(even, 1, 0), rows, :]
    two = second_ref[jnp.where(even, 0, 1), rows, :]
    return jnp.where(even, one, two), jnp.where(even, two, one)


def rotate(x, shift):
    shift %= 128
    return pltpu.roll(x, shift, 1) if shift else x


def edge_kernel(
    first_ref, second_ref, held_ref, weight_ref, offset_ref,
    rows_b_ref, rows_c_ref, send_ref, strip_ref, coeff_ref,
):
    sec = lax.axis_index("sec")
    grp = lax.axis_index("grp")
    even = sec % 2 == 0
    lane = lanes((8, 128))

    def side(right, left, count):
        return jnp.where(lane < count, right, jnp.where(lane >= 128 - EDGE, left, 0.0))

    for a in range(FIELDS + 1):
        start, place = spot(a)
        right, left = neighbours(even, first_ref, second_ref, slice(128 + 8 * (a // 4), 136 + 8 * (a // 4)))
        top = 32 * (a % 4)
        high = jnp.concatenate(
            [held_ref[a, 248:256, :], side(rotate(right, -top), rotate(left, 96 - top), WIDE)], axis=1
        )
        right, left = neighbours(even, first_ref, second_ref, pl.ds(start, 8, stride=8))
        low = jnp.concatenate(
            [held_ref[a, 0:8, :], side(rotate(right, -place), rotate(left, -EDGE - place), EDGE)], axis=1
        )
        right, left = neighbours(even, first_ref, second_ref, pl.ds(start + 7, 8, stride=8))
        place = place + 64
        strip_ref[a, 0:8, 0:128] = held_ref[a, 240:248, :]
        strip_ref[a, 0:8, 128:256] = side(rotate(right, -place), rotate(left, -EDGE - place), EDGE)
        strip_ref[a, 8:16, :] = high
        rows_b_ref[a] = jnp.where(grp % 2 == 0, high, low)
        rows_c_ref[a] = jnp.where(grp == 2, low, high)
        if a < FIELDS:
            send_ref[2 * a : 2 * a + 1, :] = high[7:8, :]
            send_ref[2 * a + 1 : 2 * a + 2, :] = high[6:7, :]
    send_ref[10:16, :] = jnp.zeros((6, 256), jnp.float32)

    sectors = weight_ref.shape[1] // 128

    def window(ref, which):
        start = pl.multiple_of(((sec + which + sectors) % sectors) * 128, 128)
        return ref[:, pl.ds(start, 128)]

    def extended(ref):
        near, right, left = (window(ref, k) for k in (0, 1, -1))
        return jnp.concatenate([near, jnp.where(lanes(right.shape) < 64, right, left)], axis=1)

    weight = extended(weight_ref)
    total = weight[0:1] + weight[1:2] + weight[2:3] + weight[3:4]
    weight = weight / total
    offset = extended(offset_ref)
    for distance in range(2 * DONORS - 1):
        coeff = jnp.zeros((1, 256), jnp.float32)
        for k in range(DONORS):
            coeff = coeff + jnp.where(offset == distance - k, weight[k : k + 1], 0.0)
        coeff_ref[distance : distance + 1, :] = coeff
    coeff_ref[7:8, :] = jnp.zeros((1, 256), jnp.float32)


def layers_of(got_ref):
    return got_ref[...] if len(got_ref.shape) == 2 else got_ref[1 - lax.axis_index("row")]


def strip_stage(now_ref, got_ref, strip_ref, coeff_ref, matrices_ref, rows_ref, blocks, sides):
    ghost = ghost_layers(layers_of(got_ref), coeff_ref)
    for f in range(FIELDS):
        rows_ref[f, 0:8, :] = jnp.zeros((8, 256), jnp.float32)
        rows_ref[f, 8:24, :] = now_ref[f]
        rows_ref[f, 24:26, :] = ghost[2 * f : 2 * f + 2, :]
        rows_ref[f, 26:32, :] = jnp.zeros((6, 256), jnp.float32)

    def halves(h):
        return slice(128 * h, 128 * (h + 1))

    return [
        both(
            lambda f, k, h: rows_ref[f, 8 + 8 * b + k : 16 + 8 * b + k, halves(h)],
            lambda h: strip_ref[FIELDS, 8 * b : 8 * b + 8, halves(h)],
            matrices_ref,
            sides,
        )
        for b in blocks
    ]


def strip_kernel(stage, matrices_ref, coeff_ref, got_ref, strip_ref, *refs):
    now_ref, out_ref, send_ref, rows_ref = refs if stage else (strip_ref, *refs)
    new = strip_stage(now_ref, got_ref, strip_ref, coeff_ref, matrices_ref, rows_ref, (0, 1), 2)
    for b in range(2):
        for h in range(2):
            for f in range(FIELDS):
                place = f, slice(8 * b, 8 * b + 8), slice(128 * h, 128 * h + 128)
                value = new[b][h][f]
                if stage:
                    value = 0.75 * strip_ref[place] + 0.25 * value
                out_ref[place] = value
                if b:
                    send_ref[2 * f : 2 * f + 1, place[2]] = value[7:8, :]
                    send_ref[2 * f + 1 : 2 * f + 2, place[2]] = value[6:7, :]
    send_ref[10:16, :] = jnp.zeros((6, 256), jnp.float32)


def last_kernel(matrices_ref, coeff_ref, got_ref, strip_ref, now_ref, _, out_ref, rows_ref, new_ref, sem):
    ((new,),) = strip_stage(now_ref, got_ref, strip_ref, coeff_ref, matrices_ref, rows_ref, (1,), 1)
    for f in range(FIELDS):
        new_ref[f] = strip_ref[f, 8:16, 0:128] / 3.0 + (2.0 / 3.0) * new[f]

    @pl.when(lax.axis_index("grp") == 3)
    def _():
        copy = pltpu.make_async_copy(new_ref, out_ref.at[0, :, 248:256, :], sem)
        copy.start()
        copy.wait()


def block_kernel(
    matrices_ref, first_ref, second_ref, own_ref, rows_b_ref, rows_c_ref, held_ref,
    out_ref, x_ref, y_ref, z_ref, d_ref, gx_ref, gy_ref, gz_ref, ge_ref, gd_ref,
):
    sec = lax.axis_index("sec")
    grp = lax.axis_index("grp")
    even = sec % 2 == 0
    lane = lanes((8, 128))
    part = lane % 32
    row = lax.broadcasted_iota(jnp.int32, (8, 128), 0)

    def choose(far_left, own_left, own_right, far_right):
        return jnp.where(
            part < 16, jnp.where(part < 8, far_left, own_left), jnp.where(part < 24, own_right, far_right)
        )

    for a in range(FIELDS + 1):
        near = x_ref.at[a] if a < FIELDS else d_ref
        side = gx_ref.at[a] if a < FIELDS else gd_ref
        rows_b, rows_c = rows_b_ref[a], rows_c_ref[a]
        low = jnp.where(grp == 0, 0.0, jnp.where(grp % 2 == 1, rows_b, rows_c))
        high = jnp.where(grp == 3, 0.0, jnp.where(grp % 2 == 0, rows_b, rows_c))
        for i in range(32):
            near[REACH + i] = held_ref[a, pl.ds(i, 8, stride=32), :]
        for i in range(REACH):
            below = pltpu.roll(near[REACH + 32 - REACH + i], 1, 0)
            near[i] = jnp.where(row == 0, low[8 - REACH + i : 9 - REACH + i, 0:128], below)
            above = pltpu.roll(near[REACH + i], 7, 0)
            near[REACH + 32 + i] = jnp.where(row == 7, high[i : i + 1, 0:128], above)
        start, place = spot(a)
        for i in range(8):
            rows = slice(start + 8 * i, start + 8 * i + 8)
            right, left = neighbours(even, first_ref, second_ref, rows)
            side[REACH + i] = choose(
                rotate(left, -place),
                rotate(own_ref[0, rows, :], 8 - place),
                rotate(own_ref[1, rows, :], 16 - place),
                rotate(right, 24 - place),
            )
        low, high = (
            choose(rotate(h[:, 128:], 8), rotate(h[:, :128], 8), rotate(h[:, :128], 24), rotate(h[:, 128:], 24))
            for h in (low, high)
        )
        high = pltpu.roll(high, 96, 1)
        for i in range(REACH):
            below = pltpu.roll(side[REACH + 8 - REACH + i], 32, 1)
            below = jnp.where(lane < 32, pltpu.roll(below, 1, 0), below)
            edge = (row == 0) & (lane < 32)
            side[i] = jnp.where(edge, low[8 - REACH + i : 9 - REACH + i, :], below)
            above = pltpu.roll(side[REACH + i], 96, 1)
            above = jnp.where(lane >= 96, pltpu.roll(above, 7, 0), above)
            edge = (row == 7) & (lane >= 96)
            side[REACH + 8 + i] = jnp.where(edge, high[i : i + 1, :], above)

    def nothing_before(near, side, reach):
        @pl.when(grp == 0)
        def _():
            for f in range(FIELDS):
                for i in range(REACH - reach, REACH):
                    near[f, i, 0:1, :] = jnp.zeros((1, 128), jnp.float32)
                    side[f, i, 0:1, 0:32] = jnp.zeros((1, 32), jnp.float32)

    fields = range(FIELDS)

    def axial(ref, i):
        return ([ref[f, i + k] for f in fields] for k in (0, 1, -1, 2, -2))

    def turns(x):
        return ([pltpu.roll(v, shift, 1) for v in x] for shift in (127, 1, 126, 2))

    def near_stage(near, side_new, first, last, store):
        @pl.loop(REACH + first, REACH + last, unroll=UNROLL)
        def _(i):
            k = jnp.clip(lax.shift_right_arithmetic(i - REACH, 3), 0, 3)
            x, *others = axial(near, i)
            new = advance(x, *others, *turns(x), d_ref[i], matrices_ref)
            for f in fields:
                beside = side_new[f, i - 8 * k]
                low = pltpu.roll(beside, (120 - 32 * k) & 127, 1)
                high = pltpu.roll(beside, (104 - 32 * k) & 127, 1)
                new[f] = jnp.where(lane < 2, low, jnp.where(lane >= 126, high, new[f]))
            store(i, new)

    def side_stage(side, first, last, store):
        @pl.loop(REACH + first, REACH + last, unroll=4)
        def _(i):
            x, *others = axial(side, i)
            store(i, advance(x, *others, *turns(x), gd_ref[i], matrices_ref))

    def plain(ref):
        def store(i, new):
            for f in fields:
                ref[f, i] = new[f]

        return store

    def blended(old, weights, put):
        def store(i, new):
            for f in fields:
                put(f, i, weights[0] * old[f, i] + weights[1] * new[f])

        return store

    def into(ref):
        def put(f, i, value):
            ref[f, i] = value

        return put

    def out(f, i, value):
        out_ref[0, f, pl.ds(i - REACH, 8, stride=32), :] = value

    side_stage(gx_ref, -4, 12, plain(gy_ref))
    near_stage(x_ref, gy_ref, -4, 36, plain(y_ref))
    nothing_before(y_ref, gy_ref, 4)
    side_stage(gy_ref, -2, 10, plain(ge_ref))
    near_stage(y_ref, ge_ref, -2, 34, blended(x_ref, (0.75, 0.25), into(z_ref)))
    for i in range(REACH - 2, REACH + 10):
        for f in fields:
            gz_ref[f, i] = 0.75 * gx_ref[f, i] + 0.25 * ge_ref[f, i]
    nothing_before(z_ref, gz_ref, 2)
    side_stage(gz_ref, 0, 8, plain(ge_ref))
    near_stage(z_ref, ge_ref, 0, 32, blended(x_ref, (1.0 / 3.0, 2.0 / 3.0), out))


def call(kernel, in_specs, out_shapes, scratch=(), out_specs=None, flops=0, vmem=40, **options):
    return pl.pallas_call(
        kernel,
        in_specs=in_specs,
        out_specs=out_specs or [SMEM if s == ROUTE else VMEM for s in out_shapes],
        out_shape=[jax.ShapeDtypeStruct(s, jnp.int32 if s == ROUTE else jnp.float32) for s in out_shapes],
        scratch_shapes=list(scratch),
        compiler_params=pltpu.CompilerParams(vmem_limit_bytes=vmem * 1024 * 1024),
        cost_estimate=pl.CostEstimate(flops=flops, bytes_accessed=flops // 10, transcendentals=0) if flops else None,
        **options,
    )


def solution(mesh):
    groups, sectors = mesh.shape["grp"], mesh.shape["sec"]

    def device(row, grp, sec):
        return (row * groups + grp) * sectors + sec % sectors

    everywhere = [(r, g) for r in range(2) for g in range(groups)]
    cores = [
        [device(r, g, c), device(r, g, c + 1)] for r, g in everywhere for c in range(0, sectors, 2)
    ]
    chips = [
        [device(r, g, c), device(r, g, c + 1)] for r, g in everywhere for c in range(1, sectors, 2)
    ]

    def swap(lows):
        pairs = []
        for r in range(2):
            for g in lows:
                for c in range(sectors):
                    one, two = device(r, g, c), device(r, g + 1, c)
                    pairs += [(one, two), (two, one)]
        return pairs

    def across(shift):
        pairs = [[device(0, groups - 1, c), device(1, groups - 1, c + shift)] for c in range(sectors)]
        return pairs + [
            [device(r, g, c), device(r, g, c + 1)]
            for r, g in everywhere
            if g < groups - 1
            for c in range(0, sectors, 2)
        ]

    def gather(x, members):
        return lax.all_gather(x, AXES, axis_index_groups=members)

    half = sectors // 2
    opposite = [pair for one, two in across(half)[:sectors] for pair in ((one, two), (two, one))]

    def branch(shift):
        if shift == half:
            return lambda x: jnp.stack([lax.ppermute(x, AXES, opposite)] * 2)
        return lambda x: gather(x, across(shift))

    branches = [branch(s) for s in range(0, sectors - 2, 2)] + [branch(sectors - 1)]

    def moved(got, back):
        row, even = lax.axis_index("row"), lax.axis_index("sec") % 2 == 0
        mine = jnp.where(row == 0, got[1], got[0])
        one, two = gather(mine, cores), gather(mine, chips)
        ahead = jnp.where(even, one[1], two[1])
        behind = jnp.where(even, two[0], one[0])
        result = jnp.where((row == 0) != (back == 1), ahead, behind)
        return jnp.stack([result, result])

    def any_shift(send, nearest, exact, back):
        got = lax.switch(nearest, branches, send)
        return lax.switch(exact, [lambda got: moved(got, back), lambda got: got], got)

    arrays = FIELDS + 1
    strip_shape = (FIELDS, 16, 256)
    rows = pltpu.VMEM((FIELDS, 32, 256), jnp.float32)

    def variant(at_half, at_last):
        def run(
            nearest, exact, back, send,
            strip, coeff, matrices, first, second, own, rows_b, rows_c, held,
        ):
            rows_b = lax.ppermute(rows_b, AXES, swap((0, 2)))
            rows_c = lax.ppermute(rows_c, AXES, swap((1,)))
            now = ()
            for stage in range(3):
                if stage == at_half:
                    got = lax.ppermute(send, AXES, opposite)
                    near = (32 + 2 * REACH, 8, 128)
                    side = (8 + 2 * REACH, 8, 128)
                    shapes = [(FIELDS, *near)] * 3 + [near] + [(FIELDS, *side)] * 4 + [side]
                    send, rows_b = lax.optimization_barrier((send, rows_b))
                    (block,) = call(
                        block_kernel,
                        [VMEM] * 7,
                        [(1, FIELDS, 256, 128)],
                        [pltpu.VMEM(shape, jnp.float32) for shape in shapes],
                        flops=40_000_000,
                    )(matrices, first, second, own, rows_b, rows_c, held)
                    got, block = lax.optimization_barrier((got, block))
                elif stage == at_last:
                    got = gather(send, across(sectors - 1))
                else:
                    got = any_shift(send, nearest, exact, back)
                if stage < 2:
                    strip_now, send = call(
                        functools.partial(strip_kernel, stage),
                        [VMEM] * (4 + len(now)),
                        [strip_shape, (16, 256)],
                        [rows],
                    )(matrices, coeff, got, strip, *now)
                    now = (strip_now,)
            (out,) = call(
                last_kernel,
                [VMEM] * 5 + [ANY],
                [(1, FIELDS, 256, 128)],
                [rows, pltpu.VMEM((FIELDS, 8, 128), jnp.float32), pltpu.SemaphoreType.DMA],
                [ANY],
                input_output_aliases={5: 0},
            )(matrices, coeff, got, strip, *now, block)
            return out

        return run

    variants = [variant(i, j) for i in range(3) for j in range(3) if i != j]

    def shards(state, damping, jac_axial, jac_angular, section_shift, donor_offset, match_weight):
        first, second, held, own, matrices, *route = call(
            pack_kernel,
            [HBM] * 5,
            [(144, 128)] * 2 + [(arrays, 256, 128), (2, 128, 128), (2 * ENTRIES, 8, 128)] + [ROUTE] * 4,
            [
                pltpu.VMEM((2, FIELDS, 1, FIELDS), jnp.float32),
                pltpu.SMEM((3,), jnp.int32),
                pltpu.SemaphoreType.DMA((arrays + 3,)),
            ],
            vmem=58,
        )(state, damping, jnp.swapaxes(jac_axial, 0, 1), jnp.swapaxes(jac_angular, 0, 1), section_shift)
        which, nearest, exact, back = (r.reshape(()) for r in route)
        first = gather(first, cores)
        second = gather(second, chips)
        rows_b, rows_c, send, strip, coeff = call(
            edge_kernel,
            [VMEM] * 5,
            [(arrays, 8, 256)] * 2 + [(16, 256), (arrays, 16, 256), (8, 256)],
        )(first, second, held, match_weight, donor_offset[None, :])
        return lax.switch(
            which, variants, nearest, exact, back, send,
            strip, coeff, matrices, first, second, own, rows_b, rows_c, held,
        )

    return jax.shard_map(
        shards,
        mesh=mesh,
        in_specs=(
            P("row", None, "grp", "sec"),
            P("row", "grp", "sec"),
            P("row", None, None),
            P("row", None, None),
            P(),
            P(),
            P(),
        ),
        out_specs=P("row", None, "grp", "sec"),
        check_vma=False,
    )
```

```python
import functools

import jax
import jax.numpy as jnp
from jax import lax
from jax.experimental import pallas as pl
from jax.experimental.pallas import tpu as pltpu
from jax.sharding import PartitionSpec as P

DONORS = 4
FIELDS = 5
STEP = 0.3
VISCOSITY = 0.05
AXES = ("row", "grp", "sec")

EDGE = 8
WIDE = 24
SECTORS = 64
ROUTE = (1,)
UNROLL = 8
REACH = 6

VMEM = pl.BlockSpec(memory_space=pltpu.VMEM)
ANY = pl.BlockSpec(memory_space=pl.ANY)
HBM = pl.BlockSpec(memory_space=pltpu.HBM)
SMEM = pl.BlockSpec(memory_space=pltpu.SMEM)


def lanes(shape):
    return lax.broadcasted_iota(jnp.int32, shape, len(shape) - 1)


def unique(i, j):
    i, j = min(i, j), max(i, j)
    return i * FIELDS - i * (i - 1) // 2 + j - i


ENTRIES = FIELDS * (FIELDS + 1) // 2


def advance(x, up1, down1, up2, down2, right1, left1, right2, left2, damping, matrices_ref):
    fields = range(FIELDS)
    grad_q = [(up1[f] - down1[f]) - 0.125 * (up2[f] - down2[f]) for f in fields]
    grad_t = [(right1[f] - left1[f]) - 0.125 * (right2[f] - left2[f]) for f in fields]
    keep = (1.0 - 4.0 * STEP * VISCOSITY) - STEP * damping
    results = []
    for i in fields:
        flux = None
        for j in fields:
            term = matrices_ref[unique(i, j)] * grad_q[j] + matrices_ref[ENTRIES + unique(i, j)] * grad_t[j]
            flux = term if flux is None else flux + term
        lap = (up1[i] + down1[i]) + (right1[i] + left1[i])
        results.append(keep * x[i] + ((STEP * VISCOSITY) * lap - flux))
    return results


def turned(near, side, lane):
    result = []
    for shift in (127, 1, 126, 2):
        one, two = pltpu.roll(near, shift, 1), pltpu.roll(side, shift, 1)
        inner = lane < shift if shift > 64 else lane >= shift
        result.append((jnp.where(inner, one, two), jnp.where(inner, two, one)))
    return result


def both(load, damping, matrices_ref, sides):
    fields = range(FIELDS)
    lane = lanes((8, 128))
    turns = [turned(load(f, 0, 0), load(f, 0, 1), lane) for f in fields]
    return [
        advance(
            [load(f, 0, h) for f in fields],
            *([load(f, k, h) for f in fields] for k in (1, -1, 2, -2)),
            *([turns[f][n][h] for f in fields] for n in range(4)),
            damping(h),
            matrices_ref,
        )
        for h in range(sides)
    ]


def ghost_layers(layers, coeff_ref):
    total = coeff_ref[0:1, :] * layers
    for distance in range(1, 2 * DONORS - 1):
        moved = pltpu.roll(layers, 256 - distance, 1)
        total = total + coeff_ref[distance : distance + 1, :] * moved
    return total


def spot(a):
    return 64 * (a // 4), EDGE * (a % 4)


def rotate(x, shift):
    shift %= 128
    return pltpu.roll(x, shift, 1) if shift else x


def pack_kernel(
    state_ref, damping_ref, axial_ref, angular_ref, shift_ref,
    first_ref, second_ref, held_ref, own_ref, matrices_ref,
    which_ref, nearest_ref, move_ref, jac_ref, three_ref, sems,
):
    count = FIELDS + 1
    copies = []
    for a in range(count):
        source = state_ref.at[0, a] if a < FIELDS else damping_ref.at[0]
        copies.append(pltpu.make_async_copy(source, held_ref.at[a], sems.at[a]))
    for n, ref in enumerate((axial_ref, angular_ref)):
        copies.append(pltpu.make_async_copy(ref, jac_ref.at[n], sems.at[count + n]))
    copies.append(pltpu.make_async_copy(shift_ref, three_ref, sems.at[count + 2]))
    for copy in copies[count:] + copies[:count]:
        copy.start()
    even = lax.axis_index("sec") % 2 == 0
    lane = lanes((8, 128))

    copies[count + 2].wait()
    half, last = SECTORS // 2, SECTORS - 1
    s0, s1, s2 = three_ref[0], three_ref[1], three_ref[2]
    at_half = jnp.where(s0 == half, 0, jnp.where(s1 == half, 1, 2))
    at_last = jnp.where(s0 == last, 0, jnp.where(s1 == last, 1, 2))
    free = 3 - at_half - at_last
    shift = jnp.where(free == 0, s0, jnp.where(free == 1, s1, s2))
    odd = (shift & 1) == 1
    which_ref[0] = 2 * at_half + at_last - jnp.where(at_last > at_half, 1, 0)
    by_last = (shift >= last - 1) | (shift == 0)
    nearest = jnp.where(shift == 1, 0, lax.shift_right_logical(shift, 1) - 1)
    nearest_ref[0] = jnp.where(by_last, half - 2, nearest)
    less = (shift == last - 1) | (shift == 1)
    forward = (shift == 0) | (odd & (shift != last))
    move_ref[0] = jnp.where(less, 2, jnp.where(forward, 0, 1))

    scale = STEP * 2.0 / 3.0 * 0.5
    for n in range(2):
        copies[count + n].wait()
        for i in range(FIELDS):
            for j in range(i, FIELDS):
                entry = scale * (jac_ref[n, i, :, j : j + 1] + jac_ref[n, j, :, i : i + 1])
                matrices_ref[ENTRIES * n + unique(i, j)] = jnp.broadcast_to(entry, (8, 128))

    for b in range(2):
        arrays = range(4 * b, min(4 * b + 4, count))
        for a in arrays:
            copies[a].wait()
        for i in range(8):
            low = high = jnp.zeros((8, 128), jnp.float32)
            for a in arrays:
                for k in range(4):
                    x = held_ref[a, pl.ds(8 * k + i, 8, stride=32), :]
                    place = 32 * k + spot(a)[1]
                    x = rotate(x, place)
                    low = jnp.where((lane >= place) & (lane < place + EDGE), x, low)
                    place = (place - EDGE) % 128
                    high = jnp.where((lane >= place) & (lane < place + EDGE), x, high)
            rows = slice(64 * b + 8 * i, 64 * b + 8 * i + 8)
            own_ref[0, rows, :] = low
            own_ref[1, rows, :] = high
            first_ref[rows, :] = jnp.where(even, high, low)
            second_ref[rows, :] = jnp.where(even, low, high)
        tops = jnp.zeros((8, 128), jnp.float32)
        for a in arrays:
            place = 32 * (a % 4)
            top = rotate(held_ref[a, 248:256, :], place)
            wide = (lane >= place) & (lane < place + WIDE)
            place = (place - EDGE) % 128
            tops = jnp.where(wide | ((lane >= place) & (lane < place + EDGE)), top, tops)
        first_ref[128 + 8 * b : 136 + 8 * b, :] = tops
        second_ref[128 + 8 * b : 136 + 8 * b, :] = tops


def neighbours(even, first_ref, second_ref, rows):
    one = first_ref[jnp.where(even, 1, 0), rows, :]
    two = second_ref[rows, :]
    return jnp.where(even, one, two), jnp.where(even, two, one)


def edge_kernel(
    first_ref, second_ref, held_ref, weight_ref, offset_ref,
    rows_b_ref, rows_c_ref, send_ref, strip_ref, coeff_ref,
):
    sec = lax.axis_index("sec")
    grp = lax.axis_index("grp")
    even = sec % 2 == 0
    lane = lanes((8, 128))

    def side(right, left, count):
        return jnp.where(lane < count, right, jnp.where(lane >= 128 - EDGE, left, 0.0))

    for a in range(FIELDS + 1):
        start, place = spot(a)
        right, left = neighbours(even, first_ref, second_ref, slice(128 + 8 * (a // 4), 136 + 8 * (a // 4)))
        top = 32 * (a % 4)
        high = jnp.concatenate(
            [held_ref[a, 248:256, :], side(rotate(right, -top), rotate(left, -top), WIDE)], axis=1
        )
        right, left = neighbours(even, first_ref, second_ref, pl.ds(start, 8, stride=8))
        low = jnp.concatenate(
            [held_ref[a, 0:8, :], side(rotate(right, -place), rotate(left, -place), EDGE)], axis=1
        )
        right, left = neighbours(even, first_ref, second_ref, pl.ds(start + 7, 8, stride=8))
        place = place + 64
        strip_ref[a, 0:8, 0:128] = held_ref[a, 240:248, :]
        strip_ref[a, 0:8, 128:256] = side(rotate(right, -place), rotate(left, -place), EDGE)
        strip_ref[a, 8:16, :] = high
        rows_b_ref[a] = jnp.where(grp % 2 == 0, high, low)
        rows_c_ref[a] = jnp.where(grp == 2, low, high)
        if a < FIELDS:
            send_ref[2 * a : 2 * a + 1, :] = high[7:8, :]
            send_ref[2 * a + 1 : 2 * a + 2, :] = high[6:7, :]
    send_ref[10:16, :] = jnp.zeros((6, 256), jnp.float32)

    sectors = weight_ref.shape[1] // 128

    def window(ref, which):
        start = pl.multiple_of(((sec + which + sectors) % sectors) * 128, 128)
        return ref[:, pl.ds(start, 128)]

    def extended(ref):
        near, right, left = (window(ref, k) for k in (0, 1, -1))
        return jnp.concatenate([near, jnp.where(lanes(right.shape) < 64, right, left)], axis=1)

    weight = extended(weight_ref)
    total = weight[0:1] + weight[1:2] + weight[2:3] + weight[3:4]
    weight = weight / total
    offset = extended(offset_ref)
    for distance in range(2 * DONORS - 1):
        coeff = jnp.zeros((1, 256), jnp.float32)
        for k in range(DONORS):
            coeff = coeff + jnp.where(offset == distance - k, weight[k : k + 1], 0.0)
        coeff_ref[distance : distance + 1, :] = coeff
    coeff_ref[7:8, :] = jnp.zeros((1, 256), jnp.float32)


def layers_of(got_ref):
    return got_ref[...] if len(got_ref.shape) == 2 else got_ref[1 - lax.axis_index("row")]


def strip_stage(now_ref, got_ref, strip_ref, coeff_ref, matrices_ref, rows_ref, blocks, sides):
    ghost = ghost_layers(layers_of(got_ref), coeff_ref)
    for f in range(FIELDS):
        rows_ref[f, 0:8, :] = jnp.zeros((8, 256), jnp.float32)
        rows_ref[f, 8:24, :] = now_ref[f]
        rows_ref[f, 24:26, :] = ghost[2 * f : 2 * f + 2, :]
        rows_ref[f, 26:32, :] = jnp.zeros((6, 256), jnp.float32)

    def halves(h):
        return slice(128 * h, 128 * (h + 1))

    return [
        both(
            lambda f, k, h: rows_ref[f, 8 + 8 * b + k : 16 + 8 * b + k, halves(h)],
            lambda h: strip_ref[FIELDS, 8 * b : 8 * b + 8, halves(h)],
            matrices_ref,
            sides,
        )
        for b in blocks
    ]


def strip_kernel(stage, matrices_ref, coeff_ref, got_ref, strip_ref, *refs):
    now_ref, out_ref, send_ref, rows_ref = refs if stage else (strip_ref, *refs)
    new = strip_stage(now_ref, got_ref, strip_ref, coeff_ref, matrices_ref, rows_ref, (0, 1), 2)
    for b in range(2):
        for h in range(2):
            for f in range(FIELDS):
                place = f, slice(8 * b, 8 * b + 8), slice(128 * h, 128 * h + 128)
                value = new[b][h][f]
                if stage:
                    value = 0.75 * strip_ref[place] + 0.25 * value
                out_ref[place] = value
                if b:
                    send_ref[2 * f : 2 * f + 1, place[2]] = value[7:8, :]
                    send_ref[2 * f + 1 : 2 * f + 2, place[2]] = value[6:7, :]
    send_ref[10:16, :] = jnp.zeros((6, 256), jnp.float32)


def last_kernel(matrices_ref, coeff_ref, got_ref, strip_ref, now_ref, _, out_ref, rows_ref, new_ref, sem):
    ((new,),) = strip_stage(now_ref, got_ref, strip_ref, coeff_ref, matrices_ref, rows_ref, (1,), 1)
    for f in range(FIELDS):
        new_ref[f] = strip_ref[f, 8:16, 0:128] / 3.0 + (2.0 / 3.0) * new[f]

    @pl.when(lax.axis_index("grp") == 3)
    def _():
        copy = pltpu.make_async_copy(new_ref, out_ref.at[0, :, 248:256, :], sem)
        copy.start()
        copy.wait()


def block_kernel(
    matrices_ref, first_ref, second_ref, own_ref, rows_b_ref, rows_c_ref, held_ref,
    out_ref, x_ref, y_ref, z_ref, d_ref, gx_ref, gy_ref, gz_ref, ge_ref, gd_ref,
):
    sec = lax.axis_index("sec")
    grp = lax.axis_index("grp")
    even = sec % 2 == 0
    lane = lanes((8, 128))
    part = lane % 32
    row = lax.broadcasted_iota(jnp.int32, (8, 128), 0)

    def choose(far_left, own_left, own_right, far_right):
        return jnp.where(
            part < 16, jnp.where(part < 8, far_left, own_left), jnp.where(part < 24, own_right, far_right)
        )

    for a in range(FIELDS + 1):
        near = x_ref.at[a] if a < FIELDS else d_ref
        side = gx_ref.at[a] if a < FIELDS else gd_ref
        rows_b, rows_c = rows_b_ref[a], rows_c_ref[a]
        low = jnp.where(grp == 0, 0.0, jnp.where(grp % 2 == 1, rows_b, rows_c))
        high = jnp.where(grp == 3, 0.0, jnp.where(grp % 2 == 0, rows_b, rows_c))
        for i in range(32):
            near[REACH + i] = held_ref[a, pl.ds(i, 8, stride=32), :]
        for i in range(REACH):
            below = pltpu.roll(near[REACH + 32 - REACH + i], 1, 0)
            near[i] = jnp.where(row == 0, low[8 - REACH + i : 9 - REACH + i, 0:128], below)
            above = pltpu.roll(near[REACH + i], 7, 0)
            near[REACH + 32 + i] = jnp.where(row == 7, high[i : i + 1, 0:128], above)
        start, place = spot(a)
        for i in range(8):
            rows = slice(start + 8 * i, start + 8 * i + 8)
            right, left = neighbours(even, first_ref, second_ref, rows)
            side[REACH + i] = choose(
                rotate(left, 8 - place),
                rotate(own_ref[0, rows, :], 8 - place),
                rotate(own_ref[1, rows, :], 24 - place),
                rotate(right, 24 - place),
            )
        low, high = (
            choose(rotate(h[:, 128:], 8), rotate(h[:, :128], 8), rotate(h[:, :128], 24), rotate(h[:, 128:], 24))
            for h in (low, high)
        )
        high = pltpu.roll(high, 96, 1)
        for i in range(REACH):
            below = pltpu.roll(side[REACH + 8 - REACH + i], 32, 1)
            below = jnp.where(lane < 32, pltpu.roll(below, 1, 0), below)
            edge = (row == 0) & (lane < 32)
            side[i] = jnp.where(edge, low[8 - REACH + i : 9 - REACH + i, :], below)
            above = pltpu.roll(side[REACH + i], 96, 1)
            above = jnp.where(lane >= 96, pltpu.roll(above, 7, 0), above)
            edge = (row == 7) & (lane >= 96)
            side[REACH + 8 + i] = jnp.where(edge, high[i : i + 1, :], above)

    def nothing_before(near, side, reach):
        @pl.when(grp == 0)
        def _():
            for f in range(FIELDS):
                for i in range(REACH - reach, REACH):
                    near[f, i, 0:1, :] = jnp.zeros((1, 128), jnp.float32)
                    side[f, i, 0:1, 0:32] = jnp.zeros((1, 32), jnp.float32)

    fields = range(FIELDS)

    def axial(ref, i):
        return ([ref[f, i + k] for f in fields] for k in (0, 1, -1, 2, -2))

    def turns(x):
        return ([pltpu.roll(v, shift, 1) for v in x] for shift in (127, 1, 126, 2))

    def near_stage(near, side_new, first, last, store):
        @pl.loop(REACH + first, REACH + last, unroll=UNROLL)
        def _(i):
            k = jnp.clip(lax.shift_right_arithmetic(i - REACH, 3), 0, 3)
            x, *others = axial(near, i)
            new = advance(x, *others, *turns(x), d_ref[i], matrices_ref)
            for f in fields:
                beside = side_new[f, i - 8 * k]
                low = pltpu.roll(beside, (120 - 32 * k) & 127, 1)
                high = pltpu.roll(beside, (104 - 32 * k) & 127, 1)
                new[f] = jnp.where(lane < 2, low, jnp.where(lane >= 126, high, new[f]))
            store(i, new)

    def side_stage(side, first, last, store):
        @pl.loop(REACH + first, REACH + last, unroll=4)
        def _(i):
            x, *others = axial(side, i)
            store(i, advance(x, *others, *turns(x), gd_ref[i], matrices_ref))

    def plain(ref):
        def store(i, new):
            for f in fields:
                ref[f, i] = new[f]

        return store

    def blended(old, weights, put):
        def store(i, new):
            for f in fields:
                put(f, i, weights[0] * old[f, i] + weights[1] * new[f])

        return store

    def into(ref):
        def put(f, i, value):
            ref[f, i] = value

        return put

    def out(f, i, value):
        out_ref[0, f, pl.ds(i - REACH, 8, stride=32), :] = value

    side_stage(gx_ref, -4, 12, plain(gy_ref))
    near_stage(x_ref, gy_ref, -4, 36, plain(y_ref))
    nothing_before(y_ref, gy_ref, 4)
    side_stage(gy_ref, -2, 10, plain(ge_ref))
    near_stage(y_ref, ge_ref, -2, 34, blended(x_ref, (0.75, 0.25), into(z_ref)))
    for i in range(REACH - 2, REACH + 10):
        for f in fields:
            gz_ref[f, i] = 0.75 * gx_ref[f, i] + 0.25 * ge_ref[f, i]
    nothing_before(z_ref, gz_ref, 2)
    side_stage(gz_ref, 0, 8, plain(ge_ref))
    near_stage(z_ref, ge_ref, 0, 32, blended(x_ref, (1.0 / 3.0, 2.0 / 3.0), out))


def call(kernel, in_specs, out_shapes, scratch=(), out_specs=None, flops=0, vmem=40, **options):
    return pl.pallas_call(
        kernel,
        in_specs=in_specs,
        out_specs=out_specs or [SMEM if s == ROUTE else VMEM for s in out_shapes],
        out_shape=[jax.ShapeDtypeStruct(s, jnp.int32 if s == ROUTE else jnp.float32) for s in out_shapes],
        scratch_shapes=list(scratch),
        compiler_params=pltpu.CompilerParams(vmem_limit_bytes=vmem * 1024 * 1024),
        cost_estimate=pl.CostEstimate(flops=flops, bytes_accessed=flops // 10, transcendentals=0) if flops else None,
        **options,
    )


def solution(mesh):
    groups, sectors = mesh.shape["grp"], mesh.shape["sec"]

    def device(row, grp, sec):
        return (row * groups + grp) * sectors + sec % sectors

    everywhere = [(r, g) for r in range(2) for g in range(groups)]
    cores = [
        [device(r, g, c), device(r, g, c + 1)] for r, g in everywhere for c in range(0, sectors, 2)
    ]
    chips = [
        pair
        for r, g in everywhere
        for c in range(1, sectors, 2)
        for one, two in [(device(r, g, c), device(r, g, c + 1))]
        for pair in ((one, two), (two, one))
    ]
    onward = [
        (device(r, groups - 1, c + 1 - 2 * r), device(r, groups - 1, c)) for r in range(2) for c in range(sectors)
    ]

    def swap(lows):
        pairs = []
        for r in range(2):
            for g in lows:
                for c in range(sectors):
                    one, two = device(r, g, c), device(r, g + 1, c)
                    pairs += [(one, two), (two, one)]
        return pairs

    def across(shift):
        pairs = [[device(0, groups - 1, c), device(1, groups - 1, c + shift)] for c in range(sectors)]
        return pairs + [
            [device(r, g, c), device(r, g, c + 1)]
            for r, g in everywhere
            if g < groups - 1
            for c in range(0, sectors, 2)
        ]

    def gather(x, members):
        return lax.all_gather(x, AXES, axis_index_groups=members)

    half = sectors // 2
    opposite = [pair for one, two in across(half)[:sectors] for pair in ((one, two), (two, one))]

    def branch(shift):
        if shift == half:
            return lambda x: jnp.stack([lax.ppermute(x, AXES, opposite)] * 2)
        return lambda x: gather(x, across(shift))

    branches = [branch(s) for s in range(2, sectors - 2, 2)] + [branch(sectors - 1)]

    def mine(got):
        return jnp.where(lax.axis_index("row") == 0, got[1], got[0])

    def forth(got):
        return jnp.stack([lax.ppermute(mine(got), AXES, onward)] * 2)

    def back(got):
        row, even = lax.axis_index("row"), lax.axis_index("sec") % 2 == 0
        one, two = gather(mine(got), cores), lax.ppermute(mine(got), AXES, chips)
        result = jnp.where(row == 0, jnp.where(even, two, one[0]), jnp.where(even, one[1], two))
        return jnp.stack([result, result])

    def any_shift(send, nearest, move):
        got = lax.switch(nearest, branches, send)
        return lax.switch(move, [forth, lambda got: got, back], got)

    arrays = FIELDS + 1
    strip_shape = (FIELDS, 16, 256)
    rows = pltpu.VMEM((FIELDS, 32, 256), jnp.float32)

    def variant(at_half, at_last):
        def run(
            nearest, move, send,
            strip, coeff, matrices, first, second, own, rows_b, rows_c, held,
        ):
            rows_b = lax.ppermute(rows_b, AXES, swap((0, 2)))
            rows_c = lax.ppermute(rows_c, AXES, swap((1,)))
            now = ()
            for stage in range(3):
                if stage == at_half:
                    got = lax.ppermute(send, AXES, opposite)
                    near = (32 + 2 * REACH, 8, 128)
                    side = (8 + 2 * REACH, 8, 128)
                    shapes = [(FIELDS, *near)] * 3 + [near] + [(FIELDS, *side)] * 4 + [side]
                    send, rows_b = lax.optimization_barrier((send, rows_b))
                    (block,) = call(
                        block_kernel,
                        [VMEM] * 7,
                        [(1, FIELDS, 256, 128)],
                        [pltpu.VMEM(shape, jnp.float32) for shape in shapes],
                        flops=40_000_000,
                    )(matrices, first, second, own, rows_b, rows_c, held)
                    got, block = lax.optimization_barrier((got, block))
                elif stage == at_last:
                    got = gather(send, across(sectors - 1))
                else:
                    got = any_shift(send, nearest, move)
                if stage < 2:
                    strip_now, send = call(
                        functools.partial(strip_kernel, stage),
                        [VMEM] * (4 + len(now)),
                        [strip_shape, (16, 256)],
                        [rows],
                    )(matrices, coeff, got, strip, *now)
                    now = (strip_now,)
            (out,) = call(
                last_kernel,
                [VMEM] * 5 + [ANY],
                [(1, FIELDS, 256, 128)],
                [rows, pltpu.VMEM((FIELDS, 8, 128), jnp.float32), pltpu.SemaphoreType.DMA],
                [ANY],
                input_output_aliases={5: 0},
            )(matrices, coeff, got, strip, *now, block)
            return out

        return run

    variants = [variant(i, j) for i in range(3) for j in range(3) if i != j]

    def shards(state, damping, jac_axial, jac_angular, section_shift, donor_offset, match_weight):
        first, second, held, own, matrices, *route = call(
            pack_kernel,
            [HBM] * 5,
            [(144, 128)] * 2 + [(arrays, 256, 128), (2, 128, 128), (2 * ENTRIES, 8, 128)] + [ROUTE] * 3,
            [
                pltpu.VMEM((2, FIELDS, 1, FIELDS), jnp.float32),
                pltpu.SMEM((3,), jnp.int32),
                pltpu.SemaphoreType.DMA((arrays + 3,)),
            ],
            vmem=58,
        )(state, damping, jnp.swapaxes(jac_axial, 0, 1), jnp.swapaxes(jac_angular, 0, 1), section_shift)
        which, nearest, move = (r.reshape(()) for r in route)
        second = lax.ppermute(second, AXES, chips)
        first = gather(first, cores)
        rows_b, rows_c, send, strip, coeff = call(
            edge_kernel,
            [VMEM] * 5,
            [(arrays, 8, 256)] * 2 + [(16, 256), (arrays, 16, 256), (8, 256)],
        )(first, second, held, match_weight, donor_offset[None, :])
        return lax.switch(
            which, variants, nearest, move, send,
            strip, coeff, matrices, first, second, own, rows_b, rows_c, held,
        )

    return jax.shard_map(
        shards,
        mesh=mesh,
        in_specs=(
            P("row", None, "grp", "sec"),
            P("row", "grp", "sec"),
            P("row", None, None),
            P("row", None, None),
            P(),
            P(),
            P(),
        ),
        out_specs=P("row", None, "grp", "sec"),
        check_vma=False,
    )
```

```python
import functools

import jax
import jax.numpy as jnp
from jax import lax
from jax.experimental import pallas as pl
from jax.experimental.pallas import tpu as pltpu
from jax.sharding import PartitionSpec as P

DONORS = 4
FIELDS = 5
STEP = 0.3
VISCOSITY = 0.05
AXES = ("row", "grp", "sec")

EDGE = 8
WIDE = 24
SECTORS = 64
ROUTE = (1,)
REACH = 6

VMEM = pl.BlockSpec(memory_space=pltpu.VMEM)
ANY = pl.BlockSpec(memory_space=pl.ANY)
HBM = pl.BlockSpec(memory_space=pltpu.HBM)
SMEM = pl.BlockSpec(memory_space=pltpu.SMEM)


def lanes(shape):
    return lax.broadcasted_iota(jnp.int32, shape, len(shape) - 1)


def unique(i, j):
    i, j = min(i, j), max(i, j)
    return i * FIELDS - i * (i - 1) // 2 + j - i


ENTRIES = FIELDS * (FIELDS + 1) // 2


def advance(x, up1, down1, up2, down2, right1, left1, right2, left2, damping, matrices_ref):
    fields = range(FIELDS)
    grad_q = [(up1[f] - down1[f]) - 0.125 * (up2[f] - down2[f]) for f in fields]
    grad_t = [(right1[f] - left1[f]) - 0.125 * (right2[f] - left2[f]) for f in fields]
    keep = (1.0 - 4.0 * STEP * VISCOSITY) - STEP * damping
    results = []
    for i in fields:
        flux = None
        for j in fields:
            term = matrices_ref[unique(i, j)] * grad_q[j] + matrices_ref[ENTRIES + unique(i, j)] * grad_t[j]
            flux = term if flux is None else flux + term
        lap = (up1[i] + down1[i]) + (right1[i] + left1[i])
        results.append(keep * x[i] + ((STEP * VISCOSITY) * lap - flux))
    return results


def turned(near, side, lane):
    result = []
    for shift in (127, 1, 126, 2):
        one, two = pltpu.roll(near, shift, 1), pltpu.roll(side, shift, 1)
        inner = lane < shift if shift > 64 else lane >= shift
        result.append((jnp.where(inner, one, two), jnp.where(inner, two, one)))
    return result


def both(load, damping, matrices_ref, sides):
    fields = range(FIELDS)
    lane = lanes((8, 128))
    turns = [turned(load(f, 0, 0), load(f, 0, 1), lane) for f in fields]
    return [
        advance(
            [load(f, 0, h) for f in fields],
            *([load(f, k, h) for f in fields] for k in (1, -1, 2, -2)),
            *([turns[f][n][h] for f in fields] for n in range(4)),
            damping(h),
            matrices_ref,
        )
        for h in range(sides)
    ]


def ghost_layers(layers, coeff_ref):
    total = coeff_ref[0:1, :] * layers
    for distance in range(1, 2 * DONORS - 1):
        moved = pltpu.roll(layers, 256 - distance, 1)
        total = total + coeff_ref[distance : distance + 1, :] * moved
    return total


def spot(a):
    return 64 * (a // 4), EDGE * (a % 4)


def rotate(x, shift):
    shift %= 128
    return pltpu.roll(x, shift, 1) if shift else x


def pack_kernel(
    state_ref, damping_ref, axial_ref, angular_ref, shift_ref,
    first_ref, second_ref, held_ref, own_ref, matrices_ref,
    which_ref, nearest_ref, move_ref, jac_ref, three_ref, sems,
):
    count = FIELDS + 1
    copies = []
    for a in range(count):
        source = state_ref.at[0, a] if a < FIELDS else damping_ref.at[0]
        copies.append(pltpu.make_async_copy(source, held_ref.at[a], sems.at[a]))
    for n, ref in enumerate((axial_ref, angular_ref)):
        copies.append(pltpu.make_async_copy(ref, jac_ref.at[n], sems.at[count + n]))
    copies.append(pltpu.make_async_copy(shift_ref, three_ref, sems.at[count + 2]))
    for copy in copies[count:] + copies[:count]:
        copy.start()
    even = lax.axis_index("sec") % 2 == 0
    lane = lanes((8, 128))

    copies[count + 2].wait()
    half, last = SECTORS // 2, SECTORS - 1
    s0, s1, s2 = three_ref[0], three_ref[1], three_ref[2]
    at_half = jnp.where(s0 == half, 0, jnp.where(s1 == half, 1, 2))
    at_last = jnp.where(s0 == last, 0, jnp.where(s1 == last, 1, 2))
    free = 3 - at_half - at_last
    shift = jnp.where(free == 0, s0, jnp.where(free == 1, s1, s2))
    odd = (shift & 1) == 1
    which_ref[0] = 2 * at_half + at_last - jnp.where(at_last > at_half, 1, 0)
    by_last = (shift >= last - 1) | (shift == 0)
    nearest = jnp.where(shift == 1, 0, lax.shift_right_logical(shift, 1) - 1)
    nearest_ref[0] = jnp.where(by_last, half - 2, nearest)
    less = (shift == last - 1) | (shift == 1)
    forward = (shift == 0) | (odd & (shift != last))
    move_ref[0] = jnp.where(less, 2, jnp.where(forward, 0, 1))

    scale = STEP * 2.0 / 3.0 * 0.5
    for n in range(2):
        copies[count + n].wait()
        for i in range(FIELDS):
            for j in range(i, FIELDS):
                entry = scale * (jac_ref[n, i, :, j : j + 1] + jac_ref[n, j, :, i : i + 1])
                matrices_ref[ENTRIES * n + unique(i, j)] = jnp.broadcast_to(entry, (8, 128))

    for b in range(2):
        arrays = range(4 * b, min(4 * b + 4, count))
        lows = [jnp.zeros((8, 128), jnp.float32)] * 8
        highs = list(lows)
        for a in arrays:
            copies[a].wait()
            for i in range(8):
                for k in range(4):
                    x = held_ref[a, pl.ds(8 * k + i, 8, stride=32), :]
                    place = 32 * k + spot(a)[1]
                    x = rotate(x, place)
                    lows[i] = jnp.where((lane >= place) & (lane < place + EDGE), x, lows[i])
                    place = (place - EDGE) % 128
                    highs[i] = jnp.where((lane >= place) & (lane < place + EDGE), x, highs[i])
        for i, (low, high) in enumerate(zip(lows, highs)):
            rows = slice(64 * b + 8 * i, 64 * b + 8 * i + 8)
            own_ref[0, rows, :] = low
            own_ref[1, rows, :] = high
            first_ref[rows, :] = jnp.where(even, high, low)
            second_ref[rows, :] = jnp.where(even, low, high)
        tops = jnp.zeros((8, 128), jnp.float32)
        for a in arrays:
            place = 32 * (a % 4)
            top = rotate(held_ref[a, 248:256, :], place)
            wide = (lane >= place) & (lane < place + WIDE)
            place = (place - EDGE) % 128
            tops = jnp.where(wide | ((lane >= place) & (lane < place + EDGE)), top, tops)
        first_ref[128 + 8 * b : 136 + 8 * b, :] = tops
        second_ref[128 + 8 * b : 136 + 8 * b, :] = tops


def neighbours(even, first_ref, second_ref, rows):
    one = first_ref[jnp.where(even, 1, 0), rows, :]
    two = second_ref[rows, :]
    return jnp.where(even, one, two), jnp.where(even, two, one)


def edge_kernel(
    first_ref, second_ref, held_ref, weight_ref, offset_ref,
    rows_b_ref, rows_c_ref, send_ref, strip_ref, coeff_ref,
):
    sec = lax.axis_index("sec")
    grp = lax.axis_index("grp")
    even = sec % 2 == 0
    lane = lanes((8, 128))

    def side(right, left, count):
        return jnp.where(lane < count, right, jnp.where(lane >= 128 - EDGE, left, 0.0))

    for a in range(FIELDS + 1):
        start, place = spot(a)
        right, left = neighbours(even, first_ref, second_ref, slice(128 + 8 * (a // 4), 136 + 8 * (a // 4)))
        top = 32 * (a % 4)
        high = jnp.concatenate(
            [held_ref[a, 248:256, :], side(rotate(right, -top), rotate(left, -top), WIDE)], axis=1
        )
        right, left = neighbours(even, first_ref, second_ref, pl.ds(start, 8, stride=8))
        low = jnp.concatenate(
            [held_ref[a, 0:8, :], side(rotate(right, -place), rotate(left, -place), EDGE)], axis=1
        )
        right, left = neighbours(even, first_ref, second_ref, pl.ds(start + 7, 8, stride=8))
        place = place + 64
        strip_ref[a, 0:8, 0:128] = held_ref[a, 240:248, :]
        strip_ref[a, 0:8, 128:256] = side(rotate(right, -place), rotate(left, -place), EDGE)
        strip_ref[a, 8:16, :] = high
        rows_b_ref[a] = jnp.where(grp % 2 == 0, high, low)
        rows_c_ref[a] = jnp.where(grp == 2, low, high)
        if a < FIELDS:
            send_ref[2 * a : 2 * a + 1, :] = high[7:8, :]
            send_ref[2 * a + 1 : 2 * a + 2, :] = high[6:7, :]
    send_ref[10:16, :] = jnp.zeros((6, 256), jnp.float32)

    sectors = weight_ref.shape[1] // 128

    def window(ref, which):
        start = pl.multiple_of(((sec + which + sectors) % sectors) * 128, 128)
        return ref[:, pl.ds(start, 128)]

    def extended(ref):
        near, right, left = (window(ref, k) for k in (0, 1, -1))
        return jnp.concatenate([near, jnp.where(lanes(right.shape) < 64, right, left)], axis=1)

    weight = extended(weight_ref)
    total = weight[0:1] + weight[1:2] + weight[2:3] + weight[3:4]
    weight = weight / total
    offset = extended(offset_ref)
    for distance in range(2 * DONORS - 1):
        coeff = jnp.zeros((1, 256), jnp.float32)
        for k in range(DONORS):
            coeff = coeff + jnp.where(offset == distance - k, weight[k : k + 1], 0.0)
        coeff_ref[distance : distance + 1, :] = coeff
    coeff_ref[7:8, :] = jnp.zeros((1, 256), jnp.float32)


def layers_of(got_ref):
    return got_ref[...] if len(got_ref.shape) == 2 else got_ref[1 - lax.axis_index("row")]


def strip_stage(now_ref, got_ref, strip_ref, coeff_ref, matrices_ref, rows_ref, blocks, sides):
    ghost = ghost_layers(layers_of(got_ref), coeff_ref)
    for f in range(FIELDS):
        rows_ref[f, 0:8, :] = jnp.zeros((8, 256), jnp.float32)
        rows_ref[f, 8:24, :] = now_ref[f]
        rows_ref[f, 24:26, :] = ghost[2 * f : 2 * f + 2, :]
        rows_ref[f, 26:32, :] = jnp.zeros((6, 256), jnp.float32)

    def halves(h):
        return slice(128 * h, 128 * (h + 1))

    return [
        both(
            lambda f, k, h: rows_ref[f, 8 + 8 * b + k : 16 + 8 * b + k, halves(h)],
            lambda h: strip_ref[FIELDS, 8 * b : 8 * b + 8, halves(h)],
            matrices_ref,
            sides,
        )
        for b in blocks
    ]


def strip_kernel(stage, matrices_ref, coeff_ref, got_ref, strip_ref, *refs):
    now_ref, out_ref, send_ref, rows_ref = refs if stage else (strip_ref, *refs)
    new = strip_stage(now_ref, got_ref, strip_ref, coeff_ref, matrices_ref, rows_ref, (0, 1), 2)
    for b in range(2):
        for h in range(2):
            for f in range(FIELDS):
                place = f, slice(8 * b, 8 * b + 8), slice(128 * h, 128 * h + 128)
                value = new[b][h][f]
                if stage:
                    value = 0.75 * strip_ref[place] + 0.25 * value
                out_ref[place] = value
                if b:
                    send_ref[2 * f : 2 * f + 1, place[2]] = value[7:8, :]
                    send_ref[2 * f + 1 : 2 * f + 2, place[2]] = value[6:7, :]
    send_ref[10:16, :] = jnp.zeros((6, 256), jnp.float32)


def last_kernel(matrices_ref, coeff_ref, got_ref, strip_ref, now_ref, _, out_ref, rows_ref, new_ref, sem):
    ((new,),) = strip_stage(now_ref, got_ref, strip_ref, coeff_ref, matrices_ref, rows_ref, (1,), 1)
    for f in range(FIELDS):
        new_ref[f] = strip_ref[f, 8:16, 0:128] / 3.0 + (2.0 / 3.0) * new[f]

    @pl.when(lax.axis_index("grp") == 3)
    def _():
        copy = pltpu.make_async_copy(new_ref, out_ref.at[0, :, 248:256, :], sem)
        copy.start()
        copy.wait()


def block_kernel(
    matrices_ref, first_ref, second_ref, own_ref, rows_b_ref, rows_c_ref, held_ref,
    out_ref, x_ref, y_ref, z_ref, d_ref, gx_ref, gy_ref, gz_ref, ge_ref, gd_ref,
):
    sec = lax.axis_index("sec")
    grp = lax.axis_index("grp")
    even = sec % 2 == 0
    lane = lanes((8, 128))
    part = lane % 32
    row = lax.broadcasted_iota(jnp.int32, (8, 128), 0)

    def choose(far_left, own_left, own_right, far_right):
        return jnp.where(
            part < 16, jnp.where(part < 8, far_left, own_left), jnp.where(part < 24, own_right, far_right)
        )

    for a in range(FIELDS + 1):
        near = x_ref.at[a] if a < FIELDS else d_ref
        side = gx_ref.at[a] if a < FIELDS else gd_ref
        rows_b, rows_c = rows_b_ref[a], rows_c_ref[a]
        low = jnp.where(grp == 0, 0.0, jnp.where(grp % 2 == 1, rows_b, rows_c))
        high = jnp.where(grp == 3, 0.0, jnp.where(grp % 2 == 0, rows_b, rows_c))
        for i in range(32):
            near[REACH + i] = held_ref[a, pl.ds(i, 8, stride=32), :]
        for i in range(REACH):
            below = pltpu.roll(near[REACH + 32 - REACH + i], 1, 0)
            near[i] = jnp.where(row == 0, low[8 - REACH + i : 9 - REACH + i, 0:128], below)
            above = pltpu.roll(near[REACH + i], 7, 0)
            near[REACH + 32 + i] = jnp.where(row == 7, high[i : i + 1, 0:128], above)
        start, place = spot(a)
        for i in range(8):
            rows = slice(start + 8 * i, start + 8 * i + 8)
            right, left = neighbours(even, first_ref, second_ref, rows)
            side[REACH + i] = choose(
                rotate(left, 8 - place),
                rotate(own_ref[0, rows, :], 8 - place),
                rotate(own_ref[1, rows, :], 24 - place),
                rotate(right, 24 - place),
            )
        low, high = (
            choose(rotate(h[:, 128:], 8), rotate(h[:, :128], 8), rotate(h[:, :128], 24), rotate(h[:, 128:], 24))
            for h in (low, high)
        )
        high = pltpu.roll(high, 96, 1)
        for i in range(REACH):
            below = pltpu.roll(side[REACH + 8 - REACH + i], 32, 1)
            below = jnp.where(lane < 32, pltpu.roll(below, 1, 0), below)
            edge = (row == 0) & (lane < 32)
            side[i] = jnp.where(edge, low[8 - REACH + i : 9 - REACH + i, :], below)
            above = pltpu.roll(side[REACH + i], 96, 1)
            above = jnp.where(lane >= 96, pltpu.roll(above, 7, 0), above)
            edge = (row == 7) & (lane >= 96)
            side[REACH + 8 + i] = jnp.where(edge, high[i : i + 1, :], above)

    def nothing_before(near, side, reach):
        @pl.when(grp == 0)
        def _():
            for f in range(FIELDS):
                for i in range(REACH - reach, REACH):
                    near[f, i, 0:1, :] = jnp.zeros((1, 128), jnp.float32)
                    side[f, i, 0:1, 0:32] = jnp.zeros((1, 32), jnp.float32)

    fields = range(FIELDS)

    def axial(ref, i):
        return ([ref[f, i + k] for f in fields] for k in (0, 1, -1, 2, -2))

    def turns(x):
        return ([pltpu.roll(v, shift, 1) for v in x] for shift in (127, 1, 126, 2))

    def near_stage(near, side_new, first, last, unroll, store):
        @pl.loop(REACH + first, REACH + last, unroll=unroll)
        def _(i):
            k = jnp.clip(lax.shift_right_arithmetic(i - REACH, 3), 0, 3)
            x, *others = axial(near, i)
            new = advance(x, *others, *turns(x), d_ref[i], matrices_ref)
            for f in fields:
                beside = side_new[f, i - 8 * k]
                low = pltpu.roll(beside, (120 - 32 * k) & 127, 1)
                high = pltpu.roll(beside, (104 - 32 * k) & 127, 1)
                new[f] = jnp.where(lane < 2, low, jnp.where(lane >= 126, high, new[f]))
            store(i, new)

    def side_stage(side, first, last, store):
        @pl.loop(REACH + first, REACH + last, unroll=4)
        def _(i):
            x, *others = axial(side, i)
            store(i, advance(x, *others, *turns(x), gd_ref[i], matrices_ref))

    def plain(ref):
        def store(i, new):
            for f in fields:
                ref[f, i] = new[f]

        return store

    def blended(old, weights, put):
        def store(i, new):
            for f in fields:
                put(f, i, weights[0] * old[f, i] + weights[1] * new[f])

        return store

    def into(ref):
        def put(f, i, value):
            ref[f, i] = value

        return put

    def out(f, i, value):
        out_ref[0, f, pl.ds(i - REACH, 8, stride=32), :] = value

    side_stage(gx_ref, -4, 12, plain(gy_ref))
    near_stage(x_ref, gy_ref, -4, 36, 10, plain(y_ref))
    nothing_before(y_ref, gy_ref, 4)
    side_stage(gy_ref, -2, 10, plain(ge_ref))
    near_stage(y_ref, ge_ref, -2, 34, 9, blended(x_ref, (0.75, 0.25), into(z_ref)))
    for i in range(REACH - 2, REACH + 10):
        for f in fields:
            gz_ref[f, i] = 0.75 * gx_ref[f, i] + 0.25 * ge_ref[f, i]
    nothing_before(z_ref, gz_ref, 2)
    side_stage(gz_ref, 0, 8, plain(ge_ref))
    near_stage(z_ref, ge_ref, 0, 32, 8, blended(x_ref, (1.0 / 3.0, 2.0 / 3.0), out))


def call(kernel, in_specs, out_shapes, scratch=(), out_specs=None, flops=0, vmem=40, **options):
    return pl.pallas_call(
        kernel,
        in_specs=in_specs,
        out_specs=out_specs or [SMEM if s == ROUTE else VMEM for s in out_shapes],
        out_shape=[jax.ShapeDtypeStruct(s, jnp.int32 if s == ROUTE else jnp.float32) for s in out_shapes],
        scratch_shapes=list(scratch),
        compiler_params=pltpu.CompilerParams(vmem_limit_bytes=vmem * 1024 * 1024),
        cost_estimate=pl.CostEstimate(flops=flops, bytes_accessed=flops // 10, transcendentals=0) if flops else None,
        **options,
    )


def solution(mesh):
    groups, sectors = mesh.shape["grp"], mesh.shape["sec"]

    def device(row, grp, sec):
        return (row * groups + grp) * sectors + sec % sectors

    everywhere = [(r, g) for r in range(2) for g in range(groups)]
    cores = [
        [device(r, g, c), device(r, g, c + 1)] for r, g in everywhere for c in range(0, sectors, 2)
    ]
    chips = [
        pair
        for r, g in everywhere
        for c in range(1, sectors, 2)
        for one, two in [(device(r, g, c), device(r, g, c + 1))]
        for pair in ((one, two), (two, one))
    ]
    onward = [
        (device(r, groups - 1, c + 1 - 2 * r), device(r, groups - 1, c)) for r in range(2) for c in range(sectors)
    ]

    def swap(lows):
        pairs = []
        for r in range(2):
            for g in lows:
                for c in range(sectors):
                    one, two = device(r, g, c), device(r, g + 1, c)
                    pairs += [(one, two), (two, one)]
        return pairs

    def across(shift):
        pairs = [[device(0, groups - 1, c), device(1, groups - 1, c + shift)] for c in range(sectors)]
        return pairs + [
            [device(r, g, c), device(r, g, c + 1)]
            for r, g in everywhere
            if g < groups - 1
            for c in range(0, sectors, 2)
        ]

    def gather(x, members):
        return lax.all_gather(x, AXES, axis_index_groups=members)

    half = sectors // 2
    opposite = [pair for one, two in across(half)[:sectors] for pair in ((one, two), (two, one))]

    def branch(shift):
        if shift == half:
            return lambda x: jnp.stack([lax.ppermute(x, AXES, opposite)] * 2)
        return lambda x: gather(x, across(shift))

    branches = [branch(s) for s in range(2, sectors - 2, 2)] + [branch(sectors - 1)]

    def mine(got):
        return jnp.where(lax.axis_index("row") == 0, got[1], got[0])

    def forth(got):
        return jnp.stack([lax.ppermute(mine(got), AXES, onward)] * 2)

    def back(got):
        row, even = lax.axis_index("row"), lax.axis_index("sec") % 2 == 0
        one, two = gather(mine(got), cores), lax.ppermute(mine(got), AXES, chips)
        result = jnp.where(row == 0, jnp.where(even, two, one[0]), jnp.where(even, one[1], two))
        return jnp.stack([result, result])

    def any_shift(send, nearest, move):
        got = lax.switch(nearest, branches, send)
        return lax.switch(move, [forth, lambda got: got, back], got)

    arrays = FIELDS + 1
    strip_shape = (FIELDS, 16, 256)
    rows = pltpu.VMEM((FIELDS, 32, 256), jnp.float32)

    def variant(at_half, at_last):
        def run(
            nearest, move, send,
            strip, coeff, matrices, first, second, own, rows_b, rows_c, held,
        ):
            rows_b = lax.ppermute(rows_b, AXES, swap((0, 2)))
            rows_c = lax.ppermute(rows_c, AXES, swap((1,)))
            now = ()
            for stage in range(3):
                if stage == at_half:
                    got = lax.ppermute(send, AXES, opposite)
                    near = (32 + 2 * REACH, 8, 128)
                    side = (8 + 2 * REACH, 8, 128)
                    shapes = [(FIELDS, *near)] * 3 + [near] + [(FIELDS, *side)] * 4 + [side]
                    send, rows_b = lax.optimization_barrier((send, rows_b))
                    (block,) = call(
                        block_kernel,
                        [VMEM] * 7,
                        [(1, FIELDS, 256, 128)],
                        [pltpu.VMEM(shape, jnp.float32) for shape in shapes],
                        flops=40_000_000,
                    )(matrices, first, second, own, rows_b, rows_c, held)
                    got, block = lax.optimization_barrier((got, block))
                elif stage == at_last:
                    got = gather(send, across(sectors - 1))
                else:
                    got = any_shift(send, nearest, move)
                if stage < 2:
                    strip_now, send = call(
                        functools.partial(strip_kernel, stage),
                        [VMEM] * (4 + len(now)),
                        [strip_shape, (16, 256)],
                        [rows],
                    )(matrices, coeff, got, strip, *now)
                    now = (strip_now,)
            (out,) = call(
                last_kernel,
                [VMEM] * 5 + [ANY],
                [(1, FIELDS, 256, 128)],
                [rows, pltpu.VMEM((FIELDS, 8, 128), jnp.float32), pltpu.SemaphoreType.DMA],
                [ANY],
                input_output_aliases={5: 0},
            )(matrices, coeff, got, strip, *now, block)
            return out

        return run

    variants = [variant(i, j) for i in range(3) for j in range(3) if i != j]

    def shards(state, damping, jac_axial, jac_angular, section_shift, donor_offset, match_weight):
        first, second, held, own, matrices, *route = call(
            pack_kernel,
            [HBM] * 5,
            [(144, 128)] * 2 + [(arrays, 256, 128), (2, 128, 128), (2 * ENTRIES, 8, 128)] + [ROUTE] * 3,
            [
                pltpu.VMEM((2, FIELDS, 1, FIELDS), jnp.float32),
                pltpu.SMEM((3,), jnp.int32),
                pltpu.SemaphoreType.DMA((arrays + 3,)),
            ],
            vmem=58,
        )(state, damping, jnp.swapaxes(jac_axial, 0, 1), jnp.swapaxes(jac_angular, 0, 1), section_shift)
        which, nearest, move = (r.reshape(()) for r in route)
        second = lax.ppermute(second, AXES, chips)
        first = gather(first, cores)
        rows_b, rows_c, send, strip, coeff = call(
            edge_kernel,
            [VMEM] * 5,
            [(arrays, 8, 256)] * 2 + [(16, 256), (arrays, 16, 256), (8, 256)],
        )(first, second, held, match_weight, donor_offset[None, :])
        return lax.switch(
            which, variants, nearest, move, send,
            strip, coeff, matrices, first, second, own, rows_b, rows_c, held,
        )

    return jax.shard_map(
        shards,
        mesh=mesh,
        in_specs=(
            P("row", None, "grp", "sec"),
            P("row", "grp", "sec"),
            P("row", None, None),
            P("row", None, None),
            P(),
            P(),
            P(),
        ),
        out_specs=P("row", None, "grp", "sec"),
        check_vma=False,
    )
```
